512 devices in a mesh: row: 32 (over z, core), col: 16 (over y, x).
Axes of the slice: x: 4, y: 4, z: 16, core: 2. Of those that a mesh axis runs over, the one named last changes fastest.
Arguments:
- flow_tiles: bfloat16 [32, 32, 256, 256], P('row', 'col'), may hold values from 0.1 to 25
- tile_cols: int32 [32, 32], P('row', 'col'), may hold values from -1 to 31, as said below
- pairs: int32 [32768, 2], P(('row', 'col')), may hold values from -1 to 31, as said below
Outputs:
- new_flow: float32 [32, 32, 256, 256], P('row', 'col')
The draws below stay inside these ranges and needn't reach their ends.
Inputs may be any that keep to these rules, and one draw needn't show every extreme that they name: `tile_cols`: the stored slots of device (r, c) have distinct tile columns, each congruent to c modulo the col axis's size; tile row r stores tile column r. `pairs`: device (r, c) lists, in some order and without repeats, exactly the (k, s) for which slot s of the device is stored and M[r, k] and M[k, tile_cols[r, c * 2 + s]] are both stored tiles; its other rows are (-1, -1). Some device uses all 64 rows.
All inputs are finite; a program needn't handle non-finite values.
Results may differ from the reference program's by a relative error of at most 0.0003.
Values may be sent and summed in bfloat16 or wider, within the bound.
No kernel may reach another device: no remote copies, remote signals or barrier semaphores. Data moves between devices by JAX's collectives and lax.ppermute only.
A program may use at most 64 MiB of HBM per device.

```python
import jax
import jax.numpy as jnp
from jax import lax

B = 256
NB = 32
TPD = 2
PPD = 64
N_COL = 16


def draw_flow_tiles(key, part):
    second_key = jax.random.fold_in(key, 1)
    row_values = jnp.arange(NB, dtype=jnp.float32)
    row_scale = 3.0 ** (row_values / jnp.float32(max(NB - 1, 1)))
    normal_part = jnp.clip(jax.random.normal(second_key, (NB, NB, B, B), jnp.float32), -4.0, 4.0)
    magnitude = jnp.exp(0.5 * normal_part)
    return (magnitude * row_scale[:, None, None, None]).astype(jnp.bfloat16)


def block_pattern(key):
    perm_key, keep_key, row_key, col_key = jax.random.split(jax.random.fold_in(key, 11), 4)
    subkeys = jax.random.split(perm_key, NB * N_COL)
    orders = jax.vmap(lambda subkey: jax.random.permutation(subkey, TPD))(subkeys)
    columns = jnp.arange(N_COL, dtype=jnp.int32)[None, :, None] + N_COL * orders.reshape(NB, N_COL, TPD).astype(jnp.int32)
    columns = columns.reshape(NB, NB).astype(jnp.int32)
    keep = jax.random.randint(keep_key, (NB, NB), 0, 2).astype(jnp.int32) > 0
    special_row = jax.random.randint(row_key, (), 0, NB).astype(jnp.int32)
    special_col = jax.random.randint(col_key, (), 0, N_COL).astype(jnp.int32)
    special_cols = jax.lax.dynamic_slice_in_dim(columns[special_row], special_col * TPD, TPD, 0)
    indices = jnp.arange(NB, dtype=jnp.int32)
    is_special_col = jnp.any(special_cols[None, :] == indices[:, None], axis=1)
    stored = keep | (indices[:, None] == indices[None, :]) | (indices[:, None] == special_row) | is_special_col[None, :]
    slot_stored = jnp.take_along_axis(stored, columns, axis=1)
    tile_cols = jnp.where(slot_stored, columns, -1).astype(jnp.int32)
    return (columns, stored, tile_cols)


def draw_tile_cols(key, part):
    columns, stored, tile_cols = block_pattern(key)
    return tile_cols


def draw_pairs(key, part):
    columns, stored, tile_cols = block_pattern(key)
    device_cols = columns.reshape(NB, N_COL, TPD)
    slot_stored = tile_cols.reshape(NB, N_COL, TPD) >= 0
    left_ok = stored[:, None, None, :]
    right_ok = stored.T[device_cols]
    valid = slot_stored[:, :, :, None] & left_ok & right_ok
    valid = valid.reshape(NB, N_COL, PPD)
    index_list = jnp.arange(PPD, dtype=jnp.int32)
    score = jnp.where(valid, index_list, index_list + PPD).astype(jnp.int32)
    order = jnp.argsort(score, axis=-1).astype(jnp.int32)
    valid_sorted = jnp.take_along_axis(valid, order, axis=-1)
    inner_tile = jnp.where(valid_sorted, order % NB, -1)
    slot_table = jnp.where(valid_sorted, order // NB, -1)
    return jnp.stack([inner_tile, slot_table], axis=-1).reshape(NB * N_COL * PPD, 2).astype(jnp.int32)


def setup_inputs(seed: int = 0) -> dict:
    keys = jax.random.split(jax.random.key(seed), 4)
    return {
        "flow_tiles": draw_flow_tiles(jax.random.fold_in(keys[3], 71), 0),
        "tile_cols": draw_tile_cols(jax.random.fold_in(keys[3], 71), 0),
        "pairs": draw_pairs(jax.random.fold_in(keys[3], 71), 0),
    }


def reference(flow_tiles, tile_cols, pairs):
    column_ids = jnp.arange(NB, dtype=jnp.int32)
    matching = tile_cols[:, None, :] == column_ids[None, :, None]
    present = jnp.any(matching, axis=2)
    position = jnp.argmax(matching, axis=2).astype(jnp.int32)
    taken = jnp.take_along_axis(flow_tiles, position[:, :, None, None], axis=1)
    ordered = jnp.where(present[:, :, None, None], taken, jnp.zeros((), flow_tiles.dtype))
    pair_table = pairs.reshape(NB, N_COL, PPD, 2)
    slot_ids = jnp.arange(TPD, dtype=jnp.int32)

    def one_row(row_id):
        def one_device(col_id):
            inner_tile = pair_table[row_id, col_id, :, 0]
            slot_list = pair_table[row_id, col_id, :, 1]
            is_live = inner_tile >= 0
            inner_safe = jnp.maximum(inner_tile, 0)
            slot_safe = jnp.maximum(slot_list, 0)
            wanted = jnp.maximum(tile_cols[row_id, col_id * TPD + slot_safe], 0)
            left_tiles = ordered[row_id, inner_safe].astype(jnp.float32)
            right_tiles = ordered[inner_safe, wanted].astype(jnp.float32)
            products = jnp.einsum('pab,pbc->pac', left_tiles, right_tiles, precision=lax.Precision.HIGHEST)
            weight = (is_live[:, None] & (slot_list[:, None] == slot_ids[None, :])).astype(jnp.float32)
            return jnp.einsum('ps,pac->sac', weight, products, precision=lax.Precision.HIGHEST)
        return lax.map(one_device, jnp.arange(N_COL, dtype=jnp.int32))

    expanded = lax.map(one_row, jnp.arange(NB, dtype=jnp.int32)).reshape(NB, NB, B, B)
    inflated = expanded * expanded
    inflated_ordered = jnp.take_along_axis(inflated, position[:, :, None, None], axis=1)
    inflated_ordered = jnp.where(present[:, :, None, None], inflated_ordered, 0.0)
    totals = jnp.sum(inflated_ordered, axis=(0, 2))
    stored = tile_cols >= 0
    divisor = totals[jnp.maximum(tile_cols, 0)]
    divisor = jnp.where(stored[:, :, None], divisor, 1.0)
    normed = inflated * jnp.float32(NB * B) / divisor[:, :, None, :]
    blended = 0.5 * flow_tiles.astype(jnp.float32) + 0.5 * normed
    return jnp.where(stored[:, :, None, None], blended, 0.0)
```

```python
import jax
import jax.numpy as jnp
from jax import lax
from jax.experimental import pallas as pl
from jax.experimental.pallas import tpu as pltpu
from jax.sharding import Mesh, PartitionSpec as P

ROWS = ("z", "core")
COLS = ("y", "x")


def product_kernel(keep_ref, left_ref, right_ref, inflated_ref, sums_ref, total):
    step = pl.program_id(0)

    @pl.when(step == 0)
    def _():
        total[...] = jnp.zeros_like(total)

    for column in range(2):
        total[column] += jnp.dot(
            left_ref[0, 0], right_ref[0, 0, column], preferred_element_type=jnp.float32
        ) + jnp.dot(
            left_ref[0, 1], right_ref[1, 0, column], preferred_element_type=jnp.float32
        )

    @pl.when(step == pl.num_programs(0) - 1)
    def _():
        for column in range(2):
            kept = keep_ref[column] > 0
            value = total[column]
            value = jnp.where(kept, value * value, 0.0)
            inflated_ref[column] = value
            sums_ref[column : column + 1, :] = jnp.sum(value, axis=0, keepdims=True)


def block_products(keep, left, right):
    steps, _, width, _ = left.shape
    return pl.pallas_call(
        product_kernel,
        grid=(steps,),
        in_specs=[
            pl.BlockSpec(memory_space=pltpu.SMEM),
            pl.BlockSpec((1, 2, width, width), lambda i: (i, 0, 0, 0)),
            pl.BlockSpec((2, 1, 2, width, width), lambda i: (0, i, 0, 0, 0)),
        ],
        out_specs=[
            pl.BlockSpec((2, width, width), lambda i: (0, 0, 0)),
            pl.BlockSpec((2, width), lambda i: (0, 0)),
        ],
        out_shape=[
            jax.ShapeDtypeStruct((2, width, width), jnp.float32),
            jax.ShapeDtypeStruct((2, width), jnp.float32),
        ],
        scratch_shapes=[pltpu.VMEM((2, width, width), jnp.float32)],
        cost_estimate=pl.CostEstimate(
            flops=8 * steps * width**3, bytes_accessed=12 * steps * width**2, transcendentals=0
        ),
    )(keep, left, right)


def copy_for_each(shard, axis):
    length = lax.axis_size(axis)
    return lax.all_to_all(
        jnp.broadcast_to(shard[None], (length, *shard.shape)), axis, 0, 0, tiled=True
    )


def on_device(flow_tiles, tile_cols, pairs):
    width = flow_tiles.shape[3]
    col_count = lax.axis_size(COLS)
    row_count = lax.axis_size(ROWS)
    targets = lax.axis_index(COLS) + col_count * jnp.arange(2, dtype=jnp.int32)
    own = tile_cols[0]
    tiles = flow_tiles[0]
    matches = own[None, :] == targets[:, None]
    kept = jnp.any(matches, axis=1)
    zero = jnp.zeros((), tiles.dtype)
    ordered = jnp.where(
        matches[:, 0, None, None],
        tiles[0][None],
        jnp.where(matches[:, 1, None, None], tiles[1][None], zero),
    )
    right = lax.all_gather(ordered, ROWS, axis=0)
    left = copy_for_each(ordered, COLS)
    right = right.reshape(2, col_count, 2, width, width)
    inflated, sums = block_products(kept.astype(jnp.int32), left, right)
    sums = lax.all_gather(sums, "core", axis=0).sum(axis=0)
    totals = copy_for_each(sums, "z").sum(axis=0)
    totals = jnp.where(kept[:, None], totals, 1.0)
    normed = inflated * jnp.float32(row_count * width) / totals[:, None, :]
    normed = jnp.where(
        matches[0][:, None, None],
        normed[0][None],
        jnp.where(matches[1][:, None, None], normed[1][None], 0.0),
    )
    blended = 0.5 * tiles.astype(jnp.float32) + 0.5 * normed
    return jnp.where((own >= 0)[:, None, None], blended, 0.0)[None]


def solution(mesh):
    physical = Mesh(mesh.devices.reshape(16, 2, 4, 4), (*ROWS, *COLS))
    tiled = P(ROWS, COLS, None, None)
    return jax.shard_map(
        on_device,
        mesh=physical,
        in_specs=(tiled, P(ROWS, COLS), P((*ROWS, *COLS), None)),
        out_specs=tiled,
        check_vma=False,
    )
```

```python
import jax
import jax.numpy as jnp
from jax import lax
from jax.experimental import pallas as pl
from jax.experimental.pallas import tpu as pltpu
from jax.sharding import Mesh, PartitionSpec as P

ROWS = ("z", "core")
COLS = ("y", "x")
SMEM = pl.BlockSpec(memory_space=pltpu.SMEM)
VMEM = pl.BlockSpec(memory_space=pltpu.VMEM)
LIMIT = 48 * 1024 * 1024


def order_kernel(own_ref, target_ref, tiles_ref, ordered_ref):
    for place in range(2):
        target = target_ref[place]
        first = (own_ref[0] == target).astype(jnp.float32)
        second = (own_ref[1] == target).astype(jnp.float32)
        value = tiles_ref[0].astype(jnp.float32) * first + tiles_ref[1].astype(jnp.float32) * second
        ordered_ref[place] = value.astype(ordered_ref.dtype)


def product_kernel(count, guards, carried, index_ref, *refs):
    del index_ref
    lefts = refs[: 2 * count]
    rights = refs[2 * count : 4 * count]
    rest = refs[4 * count :]
    core_ref, rest = rest[0], rest[1:]
    if carried:
        for into, given in zip(rest[2:], rest[:2]):
            into[...] = given[...]
        rest = rest[2:]
    else:
        for into in rest:
            into[...] = jnp.zeros_like(into)
    for i in range(count):
        def add(i=i):
            left = [lefts[2 * i + j][0].reshape(-1, lefts[0].shape[-1]) for j in range(2)]
            left = jnp.concatenate(left, axis=1)
            half = left.shape[0] // 2
            for column in range(2):
                right = jnp.concatenate([rights[2 * i + j][column] for j in range(2)], axis=0)
                product = jnp.dot(left, right, preferred_element_type=jnp.float32)
                rest[0][column] += product[:half]
                rest[1][column] += product[half:]

        if guards[i] is None:
            add()
        else:
            pl.when(core_ref[0] == guards[i])(add)


def products(totals, left, pairs, index, core, guards):
    count = len(pairs)
    width = left.shape[-1]
    flat = [tile for pair in pairs for tile in pair]
    carried = [] if totals is None else list(totals)
    whole = pl.BlockSpec((2, width, width), lambda g, s: (0, 0, 0))

    def pick(j):
        return pl.BlockSpec((1, 2, width, width), lambda g, s: (s[j], 0, 0, 0))

    total = jax.ShapeDtypeStruct((2, width, width), jnp.float32)

    def kernel(*refs):
        product_kernel(count, guards, bool(carried), *refs)

    return pl.pallas_call(
        kernel,
        grid_spec=pltpu.PrefetchScalarGridSpec(
            num_scalar_prefetch=1,
            grid=(1,),
            in_specs=[pick(j) for j in range(2 * count)]
            + [whole] * (2 * count)
            + [SMEM]
            + [whole] * len(carried),
            out_specs=[whole, whole],
        ),
        out_shape=[total, total],
        compiler_params=pltpu.CompilerParams(vmem_limit_bytes=LIMIT),
        cost_estimate=pl.CostEstimate(
            flops=16 * count * width**3, bytes_accessed=16 * count * width**2, transcendentals=0
        ),
    )(index, *[left] * (2 * count), *flat, core, *carried)


def square_kernel(kept_ref, mine_ref, other_ref, inflated_ref, sums_ref):
    for place in range(2):
        value = mine_ref[place] + other_ref[place]
        value = jnp.where(kept_ref[place] > 0, value * value, 0.0)
        inflated_ref[place] = value
        sums_ref[place : place + 1, :] = jnp.sum(value, axis=0, keepdims=True)


def blend_kernel(scale, own_ref, target_ref, tiles_ref, inflated_ref, parts_ref, out_ref):
    totals = jnp.sum(parts_ref[...], axis=0)
    for slot in range(2):
        tile = tiles_ref[slot].astype(jnp.float32)
        for place in range(2):
            @pl.when(own_ref[slot] == target_ref[place])
            def _():
                normed = inflated_ref[place] * scale / totals[place : place + 1, :]
                out_ref[slot] = 0.5 * tile + 0.5 * normed

        @pl.when(own_ref[slot] < 0)
        def _():
            out_ref[slot] = jnp.zeros_like(tile)


def copy_for_each(shard, axis):
    length = lax.axis_size(axis)
    return lax.all_to_all(
        jnp.broadcast_to(shard[None], (length, *shard.shape)), axis, 0, 0, tiled=True
    )


def on_device(flow_tiles, tile_cols, pairs):
    width = flow_tiles.shape[3]
    planes, cores = lax.axis_size("z"), lax.axis_size("core")
    columns = lax.axis_size(COLS)
    plane, core, column = lax.axis_index("z"), lax.axis_index("core"), lax.axis_index(COLS)
    core_scalar = core.reshape(1).astype(jnp.int32)
    targets = (column + columns * jnp.arange(2, dtype=jnp.int32)).astype(jnp.int32)
    own = tile_cols[0]
    tiles = flow_tiles[0]
    tile_shape = jax.ShapeDtypeStruct((2, width, width), tiles.dtype)
    mine = pl.pallas_call(
        order_kernel, in_specs=[SMEM, SMEM, VMEM], out_specs=VMEM, out_shape=tile_shape
    )(own, targets, tiles)
    other = lax.ppermute(mine, "core", [(0, 1), (1, 0)])

    low = lax.rem(column - (2 * plane - 14) + 64, 32)
    place = jnp.where((low < 16) == (core == 0), 0, 1)
    sent = jnp.stack([jnp.where(place == 0, t[0], t[1]) for t in (mine, other)])
    left = copy_for_each(sent, COLS)

    ring = [(2 * z, 2 * ((z + 1) % planes)) for z in range(planes)]
    back = [(2 * z + 1, 2 * ((z - 1) % planes) + 1) for z in range(planes)]
    held = [(mine, other)]
    half = planes // 2
    for step in range(1, half + 1):
        perm = ring + back if step < half else back
        held.append(tuple(lax.ppermute(t, ROWS, perm) for t in held[-1]))

    def index_of(steps):
        shift = jnp.where(core == 0, -1, 1)
        out = []
        for step in steps:
            base = 2 * (plane + shift * step) + 64
            out += [lax.rem(base + core, columns), lax.rem(base + 1 - core, columns)]
        return jnp.stack(out).astype(jnp.int32)

    cut = half - 1
    first = list(range(cut))
    last = list(range(cut, half + 1))
    totals = products(
        None, left, held[:cut], index_of(first), core_scalar, [0] + [None] * (cut - 1)
    )
    totals = products(
        totals, left, held[cut:], index_of(last), core_scalar, [None] * (half - cut) + [1]
    )
    received = lax.ppermute(totals[1], "core", [(0, 1), (1, 0)])
    kept = jnp.any(own[None, :] == targets[:, None], axis=1).astype(jnp.int32)
    inflated, sums = pl.pallas_call(
        square_kernel,
        in_specs=[SMEM, VMEM, VMEM],
        out_specs=[VMEM, VMEM],
        out_shape=[
            jax.ShapeDtypeStruct((2, width, width), jnp.float32),
            jax.ShapeDtypeStruct((2, width), jnp.float32),
        ],
    )(kept, totals[0], received)
    sums = lax.all_gather(sums, "core", axis=0).sum(axis=0)
    parts = copy_for_each(sums, "z")
    scale = float(planes * cores * width)

    def blend(*refs):
        blend_kernel(scale, *refs)

    out = pl.pallas_call(
        blend,
        in_specs=[SMEM, SMEM, VMEM, VMEM, VMEM],
        out_specs=VMEM,
        out_shape=jax.ShapeDtypeStruct((2, width, width), jnp.float32),
    )(own, targets, tiles, inflated, parts)
    return out[None]


def solution(mesh):
    physical = Mesh(mesh.devices.reshape(16, 2, 4, 4), (*ROWS, *COLS))
    tiled = P(ROWS, COLS, None, None)
    return jax.shard_map(
        on_device,
        mesh=physical,
        in_specs=(tiled, P(ROWS, COLS), P((*ROWS, *COLS), None)),
        out_specs=tiled,
        check_vma=False,
    )
```

```python
import jax
import jax.numpy as jnp
from jax import lax
from jax.experimental import pallas as pl
from jax.experimental.pallas import tpu as pltpu
from jax.sharding import Mesh, PartitionSpec as P

ROWS = ("z", "core")
COLS = ("y", "x")
SMEM = pl.BlockSpec(memory_space=pltpu.SMEM)
VMEM = pl.BlockSpec(memory_space=pltpu.VMEM)
ANY = pl.BlockSpec(memory_space=pl.ANY)
HBM = pl.BlockSpec(memory_space=pltpu.HBM)
MIB = 1024 * 1024
SWAP = [(0, 1), (1, 0)]
FLOPS = 25 * 10**9


def params(mib):
    return pltpu.CompilerParams(vmem_limit_bytes=mib * MIB)


def order_kernel(own_ref, target_ref, tiles_ref, ordered_ref):
    for place in range(2):
        target = target_ref[place]
        first = (own_ref[0] == target).astype(jnp.float32)
        second = (own_ref[1] == target).astype(jnp.float32)
        value = tiles_ref[0].astype(jnp.float32) * first + tiles_ref[1].astype(jnp.float32) * second
        ordered_ref[place] = value.astype(ordered_ref.dtype)


def spread_kernel(place_ref, mine_ref, other_ref, out_ref, sems):
    place = place_ref[0]
    copies = []
    for i in range(out_ref.shape[0]):
        for j, source in enumerate((mine_ref, other_ref)):
            copies.append(
                pltpu.make_async_copy(source.at[place], out_ref.at[i, j], sems.at[i, j])
            )
    for copy in copies:
        copy.start()
    for copy in copies:
        copy.wait()


def product_kernel(groups, rows, carried, first, index_ref, guard_ref, left_ref, *refs):
    count = 2 * sum(len(g) for g, _ in groups)
    rights, refs = refs[:count], refs[count:]
    given, refs = (refs[: len(rows)], refs[len(rows) :]) if carried else ((), refs)
    totals, (held, kept, sems) = refs[: len(rows)], refs[len(rows) :]
    copies = []
    for i in range(count):
        for n, row in enumerate(rows):
            source = left_ref.at[index_ref[first + i], row]
            copies.append(pltpu.make_async_copy(source, held.at[i, n], sems.at[i, n]))
        copies.append(pltpu.make_async_copy(rights[i], kept.at[i], sems.at[i, len(rows)]))
    each = len(rows) + 1
    for copy in copies:
        copy.start()
    for n, total in enumerate(totals):
        total[...] = given[n][...] if carried else jnp.zeros_like(total)
    width = held.shape[-1]
    for copy in copies if len(groups) == 1 else []:
        copy.wait()
    for group, guard in groups:
        pairs = [2 * i + j for i in group for j in range(2)]
        for i in pairs if len(groups) > 1 else []:
            for copy in copies[each * i : each * (i + 1)]:
                copy.wait()

        def add(pairs=pairs):
            left = jnp.concatenate(
                [held[i].reshape(len(rows) * width, width) for i in pairs], axis=1
            )
            for column in range(2):
                right = jnp.concatenate([kept[i, column] for i in pairs], axis=0)
                product = jnp.dot(left, right, preferred_element_type=jnp.float32)
                for n, total in enumerate(totals):
                    total[column] += product[n * width : (n + 1) * width]

        if guard is None:
            add()
        else:
            pl.when(guard_ref[0] == guard)(add)


def index_kernel(columns, place_ref, after_ref, index_ref):
    del after_ref
    plane, core = place_ref[0], place_ref[1]
    for step in range(index_ref.shape[0] // 2):
        base = 2 * (plane + jnp.where(core == 0, -step, step)) + 2 * columns
        index_ref[2 * step] = lax.rem(base + core, columns)
        index_ref[2 * step + 1] = lax.rem(base + 1 - core, columns)


def products(totals, left, planes, index, guard, groups, rows, first=0):
    flat = [tile for pair in planes for tile in pair]
    count = len(flat)
    width = left.shape[-1]
    carried = [] if totals is None else [totals[row] for row in rows]
    total = jax.ShapeDtypeStruct((2, width, width), jnp.float32)

    def kernel(*refs):
        product_kernel(groups, rows, bool(carried), first, *refs)

    return pl.pallas_call(
        kernel,
        in_specs=[SMEM, SMEM] + [ANY] * (1 + count) + [VMEM] * len(carried),
        out_specs=[VMEM] * len(rows),
        out_shape=[total] * len(rows),
        scratch_shapes=[
            pltpu.VMEM((count, len(rows), width, width), left.dtype),
            pltpu.VMEM((count, 2, width, width), left.dtype),
            pltpu.SemaphoreType.DMA((count, len(rows) + 1)),
        ],
        compiler_params=params(14),
        cost_estimate=pl.CostEstimate(
            flops=4 * len(rows) * count * width**3,
            bytes_accessed=8 * count * width**2,
            transcendentals=0,
        ),
    )(index, guard, left, *flat, *carried)


def square_kernel(kept_ref, mine_ref, other_ref, inflated_ref, sums_ref):
    for place in range(2):
        value = mine_ref[place] + other_ref[place]
        value = jnp.where(kept_ref[place] > 0, value * value, 0.0)
        inflated_ref[place] = value
        sums_ref[place : place + 1, :] = jnp.sum(value, axis=0, keepdims=True)


def blend_kernel(scale, own_ref, target_ref, tiles_ref, inflated_ref, parts_ref, out_ref):
    totals = jnp.sum(parts_ref[...], axis=0)
    for slot in range(2):
        tile = tiles_ref[slot].astype(jnp.float32)
        for place in range(2):
            @pl.when(own_ref[slot] == target_ref[place])
            def _():
                normed = inflated_ref[place] * scale / totals[place : place + 1, :]
                out_ref[slot] = 0.5 * tile + 0.5 * normed

        @pl.when(own_ref[slot] < 0)
        def _():
            out_ref[slot] = jnp.zeros_like(tile)


def on_device(flow_tiles, tile_cols, pairs):
    width = flow_tiles.shape[3]
    planes, cores = lax.axis_size("z"), lax.axis_size("core")
    columns = lax.axis_size(COLS)
    plane, core, column = lax.axis_index("z"), lax.axis_index("core"), lax.axis_index(COLS)
    targets = (column + columns * jnp.arange(2, dtype=jnp.int32)).astype(jnp.int32)
    own = tile_cols[0]
    tiles = flow_tiles[0]
    mine = pl.pallas_call(
        order_kernel,
        in_specs=[SMEM, SMEM, VMEM],
        out_specs=VMEM,
        out_shape=jax.ShapeDtypeStruct((2, width, width), tiles.dtype),
        compiler_params=params(4),
    )(own, targets, tiles)
    other = lax.ppermute(mine, "core", SWAP)

    half = planes // 2
    ring = [(2 * z, 2 * ((z + 1) % planes)) for z in range(planes)]
    back = [(2 * z + 1, 2 * ((z - 1) % planes) + 1) for z in range(planes)]
    held = [(mine, other)]
    for step in range(1, half + 1):
        perm = ring + back if step < half else back
        held.append(tuple(lax.ppermute(t, ROWS, perm) for t in held[-1]))

    low = lax.rem(column - 2 * (plane - half + 1) + 2 * columns, 2 * columns)
    place = jnp.where((low < columns) == (core == 0), 0, 1).astype(jnp.int32).reshape(1)
    sent = pl.pallas_call(
        spread_kernel,
        in_specs=[SMEM, VMEM, VMEM],
        out_specs=HBM,
        out_shape=jax.ShapeDtypeStruct((columns, 2, width, width), tiles.dtype),
        scratch_shapes=[pltpu.SemaphoreType.DMA((columns, 2))],
        compiler_params=params(4),
    )(place, mine, other)
    left = lax.all_to_all(sent, COLS, 0, 0, tiled=True)

    core_scalar = core.astype(jnp.int32).reshape(1)

    def fill(*refs):
        index_kernel(columns, *refs)

    index = pl.pallas_call(
        fill,
        in_specs=[SMEM, ANY],
        out_specs=SMEM,
        out_shape=jax.ShapeDtypeStruct((2 * half + 2,), jnp.int32),
        compiler_params=params(1),
        cost_estimate=pl.CostEstimate(flops=FLOPS, bytes_accessed=0, transcendentals=0),
    )(jnp.stack([plane, core]).astype(jnp.int32), held[half - 1][0])
    totals = products(
        None, left, held[:half], index, core_scalar,
        [([0], 0), ([1, 2], None), ([3, 4], None), ([5, 6], None), ([7], None)], (0, 1),
    )
    outward = products(totals, left, held[half:], index, core_scalar, [([0], 1)], (1,), 2 * half)[0]
    received = lax.ppermute(outward, "core", SWAP)
    total = products(totals, left, held[half:], index, core_scalar, [([0], 1)], (0,), 2 * half)[0]
    kept = jnp.any(own[None, :] == targets[:, None], axis=1).astype(jnp.int32)
    inflated, sums = pl.pallas_call(
        square_kernel,
        in_specs=[SMEM, VMEM, VMEM],
        out_specs=[VMEM, VMEM],
        out_shape=[
            jax.ShapeDtypeStruct((2, width, width), jnp.float32),
            jax.ShapeDtypeStruct((2, width), jnp.float32),
        ],
        compiler_params=params(6),
    )(kept, total, received)
    sums = lax.all_gather(sums, "core", axis=0).sum(axis=0)
    parts = lax.all_to_all(
        jnp.broadcast_to(sums[None], (planes, *sums.shape)), "z", 0, 0, tiled=True
    )
    scale = float(planes * cores * width)

    def blend(*refs):
        blend_kernel(scale, *refs)

    out = pl.pallas_call(
        blend,
        in_specs=[SMEM, SMEM, VMEM, VMEM, VMEM],
        out_specs=VMEM,
        out_shape=jax.ShapeDtypeStruct((2, width, width), jnp.float32),
        compiler_params=params(6),
    )(own, targets, tiles, inflated, parts)
    return out[None]


def solution(mesh):
    physical = Mesh(mesh.devices.reshape(16, 2, 4, 4), (*ROWS, *COLS))
    tiled = P(ROWS, COLS, None, None)
    return jax.shard_map(
        on_device,
        mesh=physical,
        in_specs=(tiled, P(ROWS, COLS), P((*ROWS, *COLS), None)),
        out_specs=tiled,
        check_vma=False,
    )
```

```python
import functools

import jax
import jax.numpy as jnp
from jax import lax
from jax.experimental import pallas as pl
from jax.experimental.pallas import tpu as pltpu
from jax.sharding import Mesh, PartitionSpec as P

ROWS = ("z", "core")
COLS = ("y", "x")
SMEM = pl.BlockSpec(memory_space=pltpu.SMEM)
VMEM = pl.BlockSpec(memory_space=pltpu.VMEM)
ANY = pl.BlockSpec(memory_space=pl.ANY)
HBM = pl.BlockSpec(memory_space=pltpu.HBM)
MIB = 1024 * 1024
SWAP = [(0, 1), (1, 0)]
FLOPS = 26 * 10**9


def params(mib):
    return pltpu.CompilerParams(vmem_limit_bytes=mib * MIB)


def order_kernel(columns, own_ref, column_ref, tiles_ref, ordered_ref):
    for place in range(2):
        target = column_ref[0] + columns * place
        first = (own_ref[0] == target).astype(jnp.float32)
        second = (own_ref[1] == target).astype(jnp.float32)
        value = tiles_ref[0].astype(jnp.float32) * first + tiles_ref[1].astype(jnp.float32) * second
        ordered_ref[place] = value.astype(ordered_ref.dtype)


def settle_kernel(given_ref, same_ref):
    del given_ref, same_ref


def fetch(plan, guard_ref, start):
    for copies, guard in plan:
        def go(copies=copies):
            for copy in copies:
                copy.start() if start else copy.wait()

        if guard is None:
            go()
        else:
            pl.when(guard_ref[0] == guard)(go)


def product_kernel(planes, rows, groups, columns, plane_ref, core_ref, left_ref, *refs):
    count = 2 * len(planes)
    rights, refs = refs[:count], refs[count:]
    totals, (held, kept, sems) = refs[-3 - len(rows) : -3], refs[-3:]
    carried = len(refs) > 3 + len(rows)
    core = core_ref[0]
    plan = []
    for i, (distance, guard) in enumerate(planes):
        copies = []
        for j in range(2):
            inner = 2 * (plane_ref[0] + jnp.where(core == 0, -distance, distance))
            inner += jnp.where(core == 0, j, 1 - j)
            place = lax.rem(inner + 2 * columns, columns)
            for n, row in enumerate(rows):
                copies.append(
                    pltpu.make_async_copy(
                        left_ref.at[place, row], held.at[2 * i + j, n], sems.at[2 * i + j, n]
                    )
                )
            copies.append(
                pltpu.make_async_copy(
                    rights[2 * i + j], kept.at[2 * i + j], sems.at[2 * i + j, len(rows)]
                )
            )
        plan.append((copies, guard))
    for group in groups:
        fetch([plan[i] for i in group], core_ref, True)
    if not carried:
        for total in totals:
            total[...] = jnp.zeros_like(total)
    width = held.shape[-1]
    for group in groups:
        fetch([plan[i] for i in group], core_ref, False)

        def add(group=group):
            tiles = [2 * i + j for i in group for j in range(2)]
            left = jnp.concatenate(
                [held[i].reshape(len(rows) * width, width) for i in tiles], axis=1
            )
            for column in range(2):
                right = jnp.concatenate([kept[i, column] for i in tiles], axis=0)
                product = jnp.dot(left, right, preferred_element_type=jnp.float32)
                for n, total in enumerate(totals):
                    total[column] += product[n * width : (n + 1) * width]

        guard = planes[group[0]][1]
        if guard is None:
            add()
        else:
            pl.when(core == guard)(add)


def products(totals, rows, plane, core, left, held, planes, groups):
    width = left.shape[-1]
    tiles = [tile for distance, _ in planes for tile in held[distance]]
    if totals is None:
        tiles = [pltpu.with_memory_space_constraint(tile, pltpu.HBM) for tile in tiles]
    given = [] if totals is None else [totals[row] for row in rows]
    kernel = functools.partial(product_kernel, planes, rows, groups, left.shape[0])
    out = pl.pallas_call(
        kernel,
        in_specs=[SMEM, SMEM, HBM] + [HBM] * len(tiles) + [VMEM] * len(given),
        out_specs=[VMEM] * len(rows),
        out_shape=[jax.ShapeDtypeStruct((2, width, width), jnp.float32)] * len(rows),
        scratch_shapes=[
            pltpu.VMEM((len(tiles), len(rows), width, width), left.dtype),
            pltpu.VMEM((len(tiles), 2, width, width), left.dtype),
            pltpu.SemaphoreType.DMA((len(tiles), len(rows) + 1)),
        ],
        input_output_aliases={3 + len(tiles) + n: n for n in range(len(given))},
        compiler_params=params(10),
        cost_estimate=pl.CostEstimate(
            flops=4 * len(tiles) * len(rows) * width**3,
            bytes_accessed=4 * len(tiles) * (len(rows) + 2) * width**2,
            transcendentals=0,
        ),
    )(plane, core, left, *tiles, *given)
    return dict(zip(rows, out))


def square_kernel(columns, own_ref, column_ref, mine_ref, other_ref, inflated_ref, sums_ref):
    for place in range(2):
        target = column_ref[0] + columns * place
        kept = (own_ref[0] == target) | (own_ref[1] == target)
        value = mine_ref[place] + other_ref[place]
        value = jnp.where(kept, value * value, 0.0)
        inflated_ref[place] = value
        sums_ref[place : place + 1, :] = jnp.sum(value, axis=0, keepdims=True)


def blend_kernel(scale, columns, own_ref, column_ref, tiles_ref, inflated_ref, parts_ref, out_ref):
    totals = jnp.sum(parts_ref[...], axis=0)
    for slot in range(2):
        tile = tiles_ref[slot].astype(jnp.float32)
        for place in range(2):
            @pl.when(own_ref[slot] == column_ref[0] + columns * place)
            def _():
                normed = inflated_ref[place] * scale / totals[place : place + 1, :]
                out_ref[slot] = 0.5 * tile + 0.5 * normed

        @pl.when(own_ref[slot] < 0)
        def _():
            out_ref[slot] = jnp.zeros_like(tile)


def settle(value):
    return pl.pallas_call(
        settle_kernel,
        in_specs=[ANY],
        out_specs=ANY,
        out_shape=jax.ShapeDtypeStruct(value.shape, value.dtype),
        input_output_aliases={0: 0},
        compiler_params=params(1),
        cost_estimate=pl.CostEstimate(flops=FLOPS, bytes_accessed=0, transcendentals=0),
    )(value)


def on_device(flow_tiles, tile_cols, pairs):
    width = flow_tiles.shape[3]
    planes, cores = lax.axis_size("z"), lax.axis_size("core")
    columns = lax.axis_size(COLS)
    plane, core, column = lax.axis_index("z"), lax.axis_index("core"), lax.axis_index(COLS)
    plane_ref, core_ref, column_ref = (
        i.astype(jnp.int32).reshape(1) for i in (plane, core, column)
    )
    own = tile_cols[0]
    tiles = flow_tiles[0]
    mine = pl.pallas_call(
        functools.partial(order_kernel, columns),
        in_specs=[SMEM, SMEM, VMEM],
        out_specs=VMEM,
        out_shape=jax.ShapeDtypeStruct((2, width, width), tiles.dtype),
        compiler_params=params(4),
    )(own, column_ref, tiles)
    other = lax.ppermute(mine, "core", SWAP)

    half = planes // 2
    ring = [(2 * z, 2 * ((z + 1) % planes)) for z in range(planes)]
    back = [(2 * z + 1, 2 * ((z - 1) % planes) + 1) for z in range(planes)]
    held = [(mine, other)]
    for step in range(1, half + 1):
        perm = ring + back if step < half else back
        if step == half:
            held[-1] = (settle(held[-1][0]), held[-1][1])
        held.append(tuple(lax.ppermute(t, ROWS, perm) for t in held[-1]))

    low = lax.rem(column - 2 * (plane - half + 1) + 2 * columns, 2 * columns)
    place = jnp.where((low < columns) == (core == 0), 0, 1)
    sent = jnp.stack([jnp.where(place == 0, t[0], t[1]) for t in (mine, other)])
    sent = jnp.broadcast_to(sent[None], (columns, *sent.shape))
    left = lax.all_to_all(sent, COLS, 0, 0, tiled=True)

    known = (plane_ref, core_ref, left, held)
    early = [(0, 0)] + [(i, None) for i in range(1, half - 1)]
    totals = products(None, (0, 1), *known, early, [[1, 2], [3, 4], [5, 6], [0]])
    late = [(half - 1, None), (half, 1)]
    outward = products(totals, (1,), *known, late, [[0], [1]])[1]
    received = lax.ppermute(outward, "core", SWAP)
    total = products(totals, (0,), *known, late, [[0], [1]])[0]
    inflated, sums = pl.pallas_call(
        functools.partial(square_kernel, columns),
        in_specs=[SMEM, SMEM, VMEM, VMEM],
        out_specs=[VMEM, VMEM],
        out_shape=[
            jax.ShapeDtypeStruct((2, width, width), jnp.float32),
            jax.ShapeDtypeStruct((2, width), jnp.float32),
        ],
        compiler_params=params(6),
    )(own, column_ref, total, received)
    sums = lax.all_gather(sums, "core", axis=0).sum(axis=0)
    parts = lax.all_to_all(
        jnp.broadcast_to(sums[None], (planes, *sums.shape)), "z", 0, 0, tiled=True
    )
    scale = float(planes * cores * width)
    out = pl.pallas_call(
        functools.partial(blend_kernel, scale, columns),
        in_specs=[SMEM, SMEM, VMEM, VMEM, VMEM],
        out_specs=VMEM,
        out_shape=jax.ShapeDtypeStruct((2, width, width), jnp.float32),
        compiler_params=params(6),
    )(own, column_ref, tiles, inflated, parts)
    return out[None]


def solution(mesh):
    physical = Mesh(mesh.devices.reshape(16, 2, 4, 4), (*ROWS, *COLS))
    tiled = P(ROWS, COLS, None, None)
    return jax.shard_map(
        on_device,
        mesh=physical,
        in_specs=(tiled, P(ROWS, COLS), P((*ROWS, *COLS), None)),
        out_specs=tiled,
        check_vma=False,
    )
```

```python
import functools

import jax
import jax.numpy as jnp
from jax import lax
from jax.experimental import pallas as pl
from jax.experimental.pallas import tpu as pltpu
from jax.sharding import Mesh, PartitionSpec as P

ROWS = ("z", "core")
COLS = ("y", "x")
SMEM = pl.BlockSpec(memory_space=pltpu.SMEM)
VMEM = pl.BlockSpec(memory_space=pltpu.VMEM)
ANY = pl.BlockSpec(memory_space=pl.ANY)
HBM = pl.BlockSpec(memory_space=pltpu.HBM)
MIB = 1024 * 1024
SWAP = [(0, 1), (1, 0)]
FLOPS = 23 * 10**9


def params(mib):
    return pltpu.CompilerParams(vmem_limit_bytes=mib * MIB)


def order_kernel(columns, own_ref, column_ref, tiles_ref, ordered_ref):
    for place in range(2):
        target = column_ref[0] + columns * place
        first = (own_ref[0] == target).astype(jnp.float32)
        second = (own_ref[1] == target).astype(jnp.float32)
        value = tiles_ref[0].astype(jnp.float32) * first + tiles_ref[1].astype(jnp.float32) * second
        ordered_ref[place] = value.astype(ordered_ref.dtype)


def settle_kernel(given_ref, same_ref):
    del given_ref, same_ref


def fetch(plan, guard_ref, start):
    for copies, guard in plan:
        def go(copies=copies):
            for copy in copies:
                copy.start() if start else copy.wait()

        if guard is None:
            go()
        else:
            pl.when(guard_ref[0] == guard)(go)


def product_kernel(planes, rows, groups, plane_ref, core_ref, left_ref, *refs):
    count = 2 * len(planes)
    rights, refs = refs[:count], refs[count:]
    totals, (held, kept, sems) = refs[-3 - len(rows) : -3], refs[-3:]
    carried = len(refs) > 3 + len(rows)
    core = core_ref[0]
    breadth = left_ref.shape[0]
    columns = breadth * breadth
    plan = []
    for i, (distance, guard) in enumerate(planes):
        copies = []
        for j in range(2):
            inner = 2 * (plane_ref[0] + jnp.where(core == 0, -distance, distance))
            inner += jnp.where(core == 0, j, 1 - j)
            place = lax.rem(inner + 2 * columns, columns)
            y, x = place // breadth, lax.rem(place, breadth)
            outer, nested = jnp.where(core == 0, y, x), jnp.where(core == 0, x, y)
            for n, row in enumerate(rows):
                source = left_ref.at[outer, nested, row]
                copies.append(
                    pltpu.make_async_copy(source, held.at[2 * i + j, n], sems.at[2 * i + j, n])
                )
            copies.append(
                pltpu.make_async_copy(
                    rights[2 * i + j], kept.at[2 * i + j], sems.at[2 * i + j, len(rows)]
                )
            )
        plan.append((copies, guard))
    for group in groups:
        fetch([plan[i] for i in group], core_ref, True)
    if not carried:
        for total in totals:
            total[...] = jnp.zeros_like(total)
    width = held.shape[-1]
    for group in groups:
        fetch([plan[i] for i in group], core_ref, False)

        def add(group=group):
            tiles = [2 * i + j for i in group for j in range(2)]
            left = jnp.concatenate(
                [held[i].reshape(len(rows) * width, width) for i in tiles], axis=1
            )
            for column in range(2):
                right = jnp.concatenate([kept[i, column] for i in tiles], axis=0)
                product = jnp.dot(left, right, preferred_element_type=jnp.float32)
                for n, total in enumerate(totals):
                    total[column] += product[n * width : (n + 1) * width]

        guard = planes[group[0]][1]
        if guard is None:
            add()
        else:
            pl.when(core == guard)(add)


def products(totals, rows, plane, core, left, held, planes, groups):
    width = left.shape[-1]
    tiles = [tile for distance, _ in planes for tile in held[distance]]
    if totals is None:
        tiles = [pltpu.with_memory_space_constraint(tile, pltpu.HBM) for tile in tiles]
    given = [] if totals is None else [totals[row] for row in rows]
    kernel = functools.partial(product_kernel, planes, rows, groups)
    out = pl.pallas_call(
        kernel,
        in_specs=[SMEM, SMEM, HBM] + [HBM] * len(tiles) + [VMEM] * len(given),
        out_specs=[VMEM] * len(rows),
        out_shape=[jax.ShapeDtypeStruct((2, width, width), jnp.float32)] * len(rows),
        scratch_shapes=[
            pltpu.VMEM((len(tiles), len(rows), width, width), left.dtype),
            pltpu.VMEM((len(tiles), 2, width, width), left.dtype),
            pltpu.SemaphoreType.DMA((len(tiles), len(rows) + 1)),
        ],
        input_output_aliases={3 + len(tiles) + n: n for n in range(len(given))},
        compiler_params=params(10),
        cost_estimate=pl.CostEstimate(
            flops=4 * len(tiles) * len(rows) * width**3,
            bytes_accessed=4 * len(tiles) * (len(rows) + 2) * width**2,
            transcendentals=0,
        ),
    )(plane, core, left, *tiles, *given)
    return dict(zip(rows, out))


def square_kernel(columns, own_ref, column_ref, mine_ref, other_ref, inflated_ref, sums_ref):
    for place in range(2):
        target = column_ref[0] + columns * place
        kept = (own_ref[0] == target) | (own_ref[1] == target)
        value = mine_ref[place] + other_ref[place]
        value = jnp.where(kept, value * value, 0.0)
        inflated_ref[place] = value
        sums_ref[place : place + 1, :] = jnp.sum(value, axis=0, keepdims=True)


def blend_kernel(scale, columns, own_ref, column_ref, tiles_ref, inflated_ref, parts_ref, out_ref):
    totals = jnp.sum(parts_ref[...], axis=0)
    for slot in range(2):
        tile = tiles_ref[slot].astype(jnp.float32)
        for place in range(2):
            @pl.when(own_ref[slot] == column_ref[0] + columns * place)
            def _():
                normed = inflated_ref[place] * scale / totals[place : place + 1, :]
                out_ref[slot] = 0.5 * tile + 0.5 * normed

        @pl.when(own_ref[slot] < 0)
        def _():
            out_ref[slot] = jnp.zeros_like(tile)


def settle(value):
    return pl.pallas_call(
        settle_kernel,
        in_specs=[ANY],
        out_specs=ANY,
        out_shape=jax.ShapeDtypeStruct(value.shape, value.dtype),
        input_output_aliases={0: 0},
        compiler_params=params(1),
        cost_estimate=pl.CostEstimate(flops=FLOPS, bytes_accessed=0, transcendentals=0),
    )(value)


def on_device(flow_tiles, tile_cols, pairs):
    width = flow_tiles.shape[3]
    planes, cores = lax.axis_size("z"), lax.axis_size("core")
    columns = lax.axis_size(COLS)
    plane, core, column = lax.axis_index("z"), lax.axis_index("core"), lax.axis_index(COLS)
    plane_ref, core_ref, column_ref = (
        i.astype(jnp.int32).reshape(1) for i in (plane, core, column)
    )
    own = tile_cols[0]
    tiles = flow_tiles[0]
    mine = pl.pallas_call(
        functools.partial(order_kernel, columns),
        in_specs=[SMEM, SMEM, VMEM],
        out_specs=VMEM,
        out_shape=jax.ShapeDtypeStruct((2, width, width), tiles.dtype),
        compiler_params=params(4),
    )(own, column_ref, tiles)
    other = lax.ppermute(mine, "core", SWAP)

    half = planes // 2
    ring = [(2 * z, 2 * ((z + 1) % planes)) for z in range(planes)]
    back = [(2 * z + 1, 2 * ((z - 1) % planes) + 1) for z in range(planes)]
    held = [(mine, other)]
    for step in range(1, half + 1):
        perm = ring + back if step < half else back
        if step == half:
            held[-1] = (settle(held[-1][0]), held[-1][1])
        held.append(tuple(lax.ppermute(t, ROWS, perm) for t in held[-1]))

    low = lax.rem(column - 2 * (plane - half + 1) + 2 * columns, 2 * columns)
    place = jnp.where((low < columns) == (core == 0), 0, 1)
    height, breadth = lax.axis_size("y"), lax.axis_size("x")
    assert height == breadth

    def lines_of(phase):
        lines = []
        for c in range(cores):
            for fixed in range(height):
                along_x = [breadth * fixed + i for i in range(breadth)]
                along_y = [breadth * i + fixed for i in range(height)]
                line = along_x if phase == c else along_y
                lines.append([columns * c + i for i in line])
        return lines

    def copy_for_each(value, lines):
        spread = jnp.broadcast_to(value[None], (len(lines[0]), *value.shape))
        return lax.all_to_all(
            spread, ("core", *COLS), 0, 0, axis_index_groups=lines, tiled=True
        )

    sent = jnp.stack([jnp.where(place == 0, t[0], t[1]) for t in (mine, other)])
    left = copy_for_each(copy_for_each(sent, lines_of(0)), lines_of(1))

    known = (plane_ref, core_ref, left, held)
    early = [(0, 0)] + [(i, None) for i in range(1, half - 1)]
    totals = products(None, (0, 1), *known, early, [[1, 2], [3, 4], [5, 6], [0]])
    late = [(half - 1, None), (half, 1)]
    outward = products(totals, (1,), *known, late, [[0], [1]])[1]
    received = lax.ppermute(outward, "core", SWAP)
    total = products(totals, (0,), *known, late, [[0], [1]])[0]
    inflated, sums = pl.pallas_call(
        functools.partial(square_kernel, columns),
        in_specs=[SMEM, SMEM, VMEM, VMEM],
        out_specs=[VMEM, VMEM],
        out_shape=[
            jax.ShapeDtypeStruct((2, width, width), jnp.float32),
            jax.ShapeDtypeStruct((2, width), jnp.float32),
        ],
        compiler_params=params(6),
    )(own, column_ref, total, received)
    sums = lax.all_gather(sums, "core", axis=0).sum(axis=0)
    parts = lax.all_to_all(
        jnp.broadcast_to(sums[None], (planes, *sums.shape)), "z", 0, 0, tiled=True
    )
    scale = float(planes * cores * width)
    out = pl.pallas_call(
        functools.partial(blend_kernel, scale, columns),
        in_specs=[SMEM, SMEM, VMEM, VMEM, VMEM],
        out_specs=VMEM,
        out_shape=jax.ShapeDtypeStruct((2, width, width), jnp.float32),
        compiler_params=params(6),
    )(own, column_ref, tiles, inflated, parts)
    return out[None]


def solution(mesh):
    physical = Mesh(mesh.devices.reshape(16, 2, 4, 4), (*ROWS, *COLS))
    tiled = P(ROWS, COLS, None, None)
    return jax.shard_map(
        on_device,
        mesh=physical,
        in_specs=(tiled, P(ROWS, COLS), P((*ROWS, *COLS), None)),
        out_specs=tiled,
        check_vma=False,
    )
```

```python
import functools

import jax
import jax.numpy as jnp
from jax import lax
from jax.experimental import pallas as pl
from jax.experimental.pallas import tpu as pltpu
from jax.sharding import Mesh, PartitionSpec as P

ROWS = ("z", "core")
COLS = ("y", "x")
SMEM = pl.BlockSpec(memory_space=pltpu.SMEM)
VMEM = pl.BlockSpec(memory_space=pltpu.VMEM)
ANY = pl.BlockSpec(memory_space=pl.ANY)
HBM = pl.BlockSpec(memory_space=pltpu.HBM)
MIB = 1024 * 1024
SWAP = [(0, 1), (1, 0)]
SETTLE = 7
FLOPS = 26 * 10**9


def params(mib):
    return pltpu.CompilerParams(vmem_limit_bytes=mib * MIB)


def order_kernel(columns, own_ref, column_ref, tiles_ref, ordered_ref):
    for place in range(2):
        target = column_ref[0] + columns * place
        first = (own_ref[0] == target).astype(jnp.float32)
        second = (own_ref[1] == target).astype(jnp.float32)
        value = tiles_ref[0].astype(jnp.float32) * first + tiles_ref[1].astype(jnp.float32) * second
        ordered_ref[place] = value.astype(ordered_ref.dtype)


def settle_kernel(*refs):
    del refs


def fetch(plan, guard_ref, start):
    for copies, guard in plan:
        def go(copies=copies):
            for copy in copies:
                copy.start() if start else copy.wait()

        if guard is None:
            go()
        else:
            pl.when(guard_ref[0] == guard)(go)


def product_kernel(planes, rows, groups, plane_ref, core_ref, left_ref, *refs):
    count = 2 * len(planes)
    rights, refs = refs[:count], refs[count:]
    totals, (held, kept, sems) = refs[-3 - len(rows) : -3], refs[-3:]
    carried = len(refs) > 3 + len(rows)
    core = core_ref[0]
    breadth = left_ref.shape[0]
    columns = breadth * breadth
    plan = []
    for i, (distance, guard) in enumerate(planes):
        copies = []
        for j in range(2):
            inner = 2 * (plane_ref[0] + jnp.where(core == 0, -distance, distance))
            inner += jnp.where(core == 0, j, 1 - j)
            place = lax.rem(inner + 2 * columns, columns)
            y, x = place // breadth, lax.rem(place, breadth)
            outer, nested = jnp.where(core == 0, y, x), jnp.where(core == 0, x, y)
            for n, row in enumerate(rows):
                source = left_ref.at[outer, nested, row]
                copies.append(
                    pltpu.make_async_copy(source, held.at[2 * i + j, n], sems.at[2 * i + j, n])
                )
            copies.append(
                pltpu.make_async_copy(
                    rights[2 * i + j], kept.at[2 * i + j], sems.at[2 * i + j, len(rows)]
                )
            )
        plan.append((copies, guard))
    for group in groups:
        fetch([plan[i] for i in group], core_ref, True)
    if not carried:
        for total in totals:
            total[...] = jnp.zeros_like(total)
    width = held.shape[-1]
    for group in groups:
        fetch([plan[i] for i in group], core_ref, False)

        def add(group=group):
            tiles = [2 * i + j for i in group for j in range(2)]
            left = jnp.concatenate(
                [held[i].reshape(len(rows) * width, width) for i in tiles], axis=1
            )
            for column in range(2):
                right = jnp.concatenate([kept[i, column] for i in tiles], axis=0)
                product = jnp.dot(left, right, preferred_element_type=jnp.float32)
                for n, total in enumerate(totals):
                    total[column] += product[n * width : (n + 1) * width]

        guard = planes[group[0]][1]
        if guard is None:
            add()
        else:
            pl.when(core == guard)(add)


def products(totals, rows, plane, core, left, held, planes, groups):
    width = left.shape[-1]
    tiles = [tile for distance, _ in planes for tile in held[distance]]
    if totals is None:
        tiles = [pltpu.with_memory_space_constraint(tile, pltpu.HBM) for tile in tiles]
    given = [] if totals is None else [totals[row] for row in rows]
    kernel = functools.partial(product_kernel, planes, rows, groups)
    out = pl.pallas_call(
        kernel,
        in_specs=[SMEM, SMEM, HBM] + [HBM] * len(tiles) + [VMEM] * len(given),
        out_specs=[VMEM] * len(rows),
        out_shape=[jax.ShapeDtypeStruct((2, width, width), jnp.float32)] * len(rows),
        scratch_shapes=[
            pltpu.VMEM((len(tiles), len(rows), width, width), left.dtype),
            pltpu.VMEM((len(tiles), 2, width, width), left.dtype),
            pltpu.SemaphoreType.DMA((len(tiles), len(rows) + 1)),
        ],
        input_output_aliases={3 + len(tiles) + n: n for n in range(len(given))},
        compiler_params=params(10),
        cost_estimate=pl.CostEstimate(
            flops=4 * len(tiles) * len(rows) * width**3,
            bytes_accessed=4 * len(tiles) * (len(rows) + 2) * width**2,
            transcendentals=0,
        ),
    )(plane, core, left, *tiles, *given)
    return dict(zip(rows, out))


def square_kernel(columns, own_ref, column_ref, mine_ref, other_ref, inflated_ref, sums_ref):
    for place in range(2):
        target = column_ref[0] + columns * place
        kept = (own_ref[0] == target) | (own_ref[1] == target)
        value = mine_ref[place] + other_ref[place]
        value = jnp.where(kept, value * value, 0.0)
        inflated_ref[place] = value
        sums_ref[place : place + 1, :] = jnp.sum(value, axis=0, keepdims=True)


def blend_kernel(scale, columns, own_ref, column_ref, tiles_ref, inflated_ref, parts_ref, out_ref):
    totals = jnp.sum(parts_ref[...], axis=0)
    for slot in range(2):
        tile = tiles_ref[slot].astype(jnp.float32)
        for place in range(2):
            @pl.when(own_ref[slot] == column_ref[0] + columns * place)
            def _():
                normed = inflated_ref[place] * scale / totals[place : place + 1, :]
                out_ref[slot] = 0.5 * tile + 0.5 * normed

        @pl.when(own_ref[slot] < 0)
        def _():
            out_ref[slot] = jnp.zeros_like(tile)


def settle(value, *after, flops=0):
    return pl.pallas_call(
        settle_kernel,
        in_specs=[ANY] * (1 + len(after)),
        out_specs=ANY,
        out_shape=jax.ShapeDtypeStruct(value.shape, value.dtype),
        input_output_aliases={0: 0},
        compiler_params=params(1),
        cost_estimate=pl.CostEstimate(flops=flops, bytes_accessed=0, transcendentals=0),
    )(value, *after)


def on_device(flow_tiles, tile_cols, pairs):
    width = flow_tiles.shape[3]
    planes, cores = lax.axis_size("z"), lax.axis_size("core")
    columns = lax.axis_size(COLS)
    plane, core, column = lax.axis_index("z"), lax.axis_index("core"), lax.axis_index(COLS)
    plane_ref, core_ref, column_ref = (
        i.astype(jnp.int32).reshape(1) for i in (plane, core, column)
    )
    own = tile_cols[0]
    tiles = flow_tiles[0]
    mine = pl.pallas_call(
        functools.partial(order_kernel, columns),
        in_specs=[SMEM, SMEM, VMEM],
        out_specs=VMEM,
        out_shape=jax.ShapeDtypeStruct((2, width, width), tiles.dtype),
        compiler_params=params(4),
    )(own, column_ref, tiles)
    other = lax.ppermute(mine, "core", SWAP)

    half = planes // 2
    ring = [(2 * z, 2 * ((z + 1) % planes)) for z in range(planes)]
    back = [(2 * z + 1, 2 * ((z - 1) % planes) + 1) for z in range(planes)]
    low = lax.rem(column - 2 * (plane - half + 1) + 2 * columns, 2 * columns)
    place = jnp.where((low < columns) == (core == 0), 0, 1)
    height, breadth = lax.axis_size("y"), lax.axis_size("x")
    assert height == breadth

    def lines_of(phase):
        lines = []
        for c in range(cores):
            for fixed in range(height):
                along_x = [breadth * fixed + i for i in range(breadth)]
                along_y = [breadth * i + fixed for i in range(height)]
                line = along_x if phase == c else along_y
                lines.append([columns * c + i for i in line])
        return lines

    def copy_for_each(value, lines):
        spread = jnp.broadcast_to(value[None], (len(lines[0]), *value.shape))
        return lax.all_to_all(
            spread, ("core", *COLS), 0, 0, axis_index_groups=lines, tiled=True
        )

    sent = jnp.stack([jnp.where(place == 0, t[0], t[1]) for t in (mine, other)])
    left = copy_for_each(copy_for_each(sent, lines_of(0)), lines_of(1))

    held = [(mine, other)]
    totals = None
    for step in range(1, half + 1):
        if step == SETTLE:
            held[-1] = (settle(held[-1][0], flops=FLOPS), held[-1][1])
        if step == half:
            early = [(0, 0)] + [(i, None) for i in range(1, half - 1)]
            totals = products(
                None, (0, 1), plane_ref, core_ref, left, held, early, [[1, 2], [3, 4], [5, 6], [0]]
            )
            held[-1] = (settle(held[-1][0], *totals.values()), held[-1][1])
        perm = ring + back if step < half else back
        held.append(tuple(lax.ppermute(t, ROWS, perm) for t in held[-1]))
    known = (plane_ref, core_ref, left, held)
    late = [(half - 1, None), (half, 1)]
    outward = products(totals, (1,), *known, late, [[0], [1]])[1]
    received = lax.ppermute(outward, "core", SWAP)
    total = products(totals, (0,), *known, late, [[0], [1]])[0]
    inflated, sums = pl.pallas_call(
        functools.partial(square_kernel, columns),
        in_specs=[SMEM, SMEM, VMEM, VMEM],
        out_specs=[VMEM, VMEM],
        out_shape=[
            jax.ShapeDtypeStruct((2, width, width), jnp.float32),
            jax.ShapeDtypeStruct((2, width), jnp.float32),
        ],
        compiler_params=params(6),
    )(own, column_ref, total, received)
    sums = lax.all_gather(sums, "core", axis=0).sum(axis=0)
    parts = lax.all_to_all(
        jnp.broadcast_to(sums[None], (planes, *sums.shape)), "z", 0, 0, tiled=True
    )
    scale = float(planes * cores * width)
    out = pl.pallas_call(
        functools.partial(blend_kernel, scale, columns),
        in_specs=[SMEM, SMEM, VMEM, VMEM, VMEM],
        out_specs=VMEM,
        out_shape=jax.ShapeDtypeStruct((2, width, width), jnp.float32),
        compiler_params=params(6),
    )(own, column_ref, tiles, inflated, parts)
    return out[None]


def solution(mesh):
    physical = Mesh(mesh.devices.reshape(16, 2, 4, 4), (*ROWS, *COLS))
    tiled = P(ROWS, COLS, None, None)
    return jax.shard_map(
        on_device,
        mesh=physical,
        in_specs=(tiled, P(ROWS, COLS), P((*ROWS, *COLS), None)),
        out_specs=tiled,
        check_vma=False,
    )
```

```python
import functools

import jax
import jax.numpy as jnp
from jax import lax
from jax.experimental import pallas as pl
from jax.experimental.pallas import tpu as pltpu
from jax.sharding import Mesh, PartitionSpec as P

ROWS = ("z", "core")
COLS = ("y", "x")
SMEM = pl.BlockSpec(memory_space=pltpu.SMEM)
VMEM = pl.BlockSpec(memory_space=pltpu.VMEM)
ANY = pl.BlockSpec(memory_space=pl.ANY)
HBM = pl.BlockSpec(memory_space=pltpu.HBM)
MIB = 1024 * 1024
SWAP = [(0, 1), (1, 0)]
SETTLE = 8
CHAIN = 1
FLOPS = 23 * 10**9


def params(mib):
    return pltpu.CompilerParams(vmem_limit_bytes=mib * MIB)


def order_kernel(columns, own_ref, column_ref, tiles_ref, ordered_ref):
    for place in range(2):
        target = column_ref[0] + columns * place
        first = (own_ref[0] == target).astype(jnp.float32)
        second = (own_ref[1] == target).astype(jnp.float32)
        value = tiles_ref[0].astype(jnp.float32) * first + tiles_ref[1].astype(jnp.float32) * second
        ordered_ref[place] = value.astype(ordered_ref.dtype)


def settle_kernel(*refs):
    del refs


def fetch(plan, guard_ref, start):
    for copies, guard in plan:
        def go(copies=copies):
            for copy in copies:
                copy.start() if start else copy.wait()

        if guard is None:
            go()
        else:
            pl.when(guard_ref[0] == guard)(go)


def product_kernel(planes, rows, groups, plane_ref, core_ref, left_ref, *refs):
    count = 2 * len(planes)
    rights, refs = refs[:count], refs[count:]
    totals, (held, kept, sems) = refs[-3 - len(rows) : -3], refs[-3:]
    carried = len(refs) > 3 + len(rows)
    core = core_ref[0]
    breadth = left_ref.shape[0]
    columns = breadth * breadth
    plan = []
    for i, (distance, guard) in enumerate(planes):
        copies = []
        for j in range(2):
            inner = 2 * (plane_ref[0] + jnp.where(core == 0, -distance, distance))
            inner += jnp.where(core == 0, j, 1 - j)
            place = lax.rem(inner + 2 * columns, columns)
            y, x = place // breadth, lax.rem(place, breadth)
            outer, nested = jnp.where(core == 0, y, x), jnp.where(core == 0, x, y)
            for n, row in enumerate(rows):
                source = left_ref.at[outer, nested, row]
                copies.append(
                    pltpu.make_async_copy(source, held.at[2 * i + j, n], sems.at[2 * i + j, n])
                )
            copies.append(
                pltpu.make_async_copy(
                    rights[2 * i + j], kept.at[2 * i + j], sems.at[2 * i + j, len(rows)]
                )
            )
        plan.append((copies, guard))
    for group in groups:
        fetch([plan[i] for i in group], core_ref, True)
    if not carried:
        for total in totals:
            total[...] = jnp.zeros_like(total)
    width = held.shape[-1]
    for group in groups:
        fetch([plan[i] for i in group], core_ref, False)

        def add(group=group):
            tiles = [2 * i + j for i in group for j in range(2)]
            left = jnp.concatenate(
                [held[i].reshape(len(rows) * width, width) for i in tiles], axis=1
            )
            for column in range(2):
                right = jnp.concatenate([kept[i, column] for i in tiles], axis=0)
                product = jnp.dot(left, right, preferred_element_type=jnp.float32)
                for n, total in enumerate(totals):
                    total[column] += product[n * width : (n + 1) * width]

        guard = planes[group[0]][1]
        if guard is None:
            add()
        else:
            pl.when(core == guard)(add)


def products(totals, rows, plane, core, left, held, planes, groups):
    width = left.shape[-1]
    tiles = [tile for distance, _ in planes for tile in held[distance]]
    if totals is None:
        early = [pltpu.with_memory_space_constraint(tile, pltpu.HBM) for tile in tiles[:-2]]
        tiles = early + tiles[-2:]
    given = [] if totals is None else [totals[row] for row in rows]
    kernel = functools.partial(product_kernel, planes, rows, groups)
    out = pl.pallas_call(
        kernel,
        in_specs=[SMEM, SMEM, HBM] + [HBM] * len(tiles) + [VMEM] * len(given),
        out_specs=[VMEM] * len(rows),
        out_shape=[jax.ShapeDtypeStruct((2, width, width), jnp.float32)] * len(rows),
        scratch_shapes=[
            pltpu.VMEM((len(tiles), len(rows), width, width), left.dtype),
            pltpu.VMEM((len(tiles), 2, width, width), left.dtype),
            pltpu.SemaphoreType.DMA((len(tiles), len(rows) + 1)),
        ],
        input_output_aliases={3 + len(tiles) + n: n for n in range(len(given))},
        compiler_params=params(10),
        cost_estimate=pl.CostEstimate(
            flops=4 * len(tiles) * len(rows) * width**3,
            bytes_accessed=4 * len(tiles) * (len(rows) + 2) * width**2,
            transcendentals=0,
        ),
    )(plane, core, left, *tiles, *given)
    return dict(zip(rows, out))


def square_kernel(columns, own_ref, column_ref, mine_ref, other_ref, inflated_ref, sums_ref):
    for place in range(2):
        target = column_ref[0] + columns * place
        kept = (own_ref[0] == target) | (own_ref[1] == target)
        value = mine_ref[place] + other_ref[place]
        value = jnp.where(kept, value * value, 0.0)
        inflated_ref[place] = value
        sums_ref[place : place + 1, :] = jnp.sum(value, axis=0, keepdims=True)


def blend_kernel(scale, columns, own_ref, column_ref, tiles_ref, inflated_ref, parts_ref, out_ref):
    totals = jnp.sum(parts_ref[...], axis=0)
    for slot in range(2):
        tile = tiles_ref[slot].astype(jnp.float32)
        for place in range(2):
            @pl.when(own_ref[slot] == column_ref[0] + columns * place)
            def _():
                normed = inflated_ref[place] * scale / totals[place : place + 1, :]
                out_ref[slot] = 0.5 * tile + 0.5 * normed

        @pl.when(own_ref[slot] < 0)
        def _():
            out_ref[slot] = jnp.zeros_like(tile)


def settle(value, flops):
    return pl.pallas_call(
        settle_kernel,
        in_specs=[ANY],
        out_specs=ANY,
        out_shape=jax.ShapeDtypeStruct(value.shape, value.dtype),
        input_output_aliases={0: 0},
        compiler_params=params(1),
        cost_estimate=pl.CostEstimate(flops=flops, bytes_accessed=0, transcendentals=0),
    )(value)


def on_device(flow_tiles, tile_cols, pairs):
    width = flow_tiles.shape[3]
    planes, cores = lax.axis_size("z"), lax.axis_size("core")
    columns = lax.axis_size(COLS)
    plane, core, column = lax.axis_index("z"), lax.axis_index("core"), lax.axis_index(COLS)
    plane_ref, core_ref, column_ref = (
        i.astype(jnp.int32).reshape(1) for i in (plane, core, column)
    )
    own = tile_cols[0]
    tiles = flow_tiles[0]
    mine = pl.pallas_call(
        functools.partial(order_kernel, columns),
        in_specs=[SMEM, SMEM, VMEM],
        out_specs=VMEM,
        out_shape=jax.ShapeDtypeStruct((2, width, width), tiles.dtype),
        compiler_params=params(4),
    )(own, column_ref, tiles)
    other = lax.ppermute(mine, "core", SWAP)

    half = planes // 2
    ring = [(2 * z, 2 * ((z + 1) % planes)) for z in range(planes)]
    back = [(2 * z + 1, 2 * ((z - 1) % planes) + 1) for z in range(planes)]
    low = lax.rem(column - 2 * (plane - half + 1) + 2 * columns, 2 * columns)
    place = jnp.where((low < columns) == (core == 0), 0, 1)
    height, breadth = lax.axis_size("y"), lax.axis_size("x")
    assert height == breadth

    def lines_of(phase):
        lines = []
        for c in range(cores):
            for fixed in range(height):
                along_x = [breadth * fixed + i for i in range(breadth)]
                along_y = [breadth * i + fixed for i in range(height)]
                line = along_x if phase == c else along_y
                lines.append([columns * c + i for i in line])
        return lines

    def copy_for_each(value, lines):
        spread = jnp.broadcast_to(value[None], (len(lines[0]), *value.shape))
        return lax.all_to_all(
            spread, ("core", *COLS), 0, 0, axis_index_groups=lines, tiled=True
        )

    sent = jnp.stack([jnp.where(place == 0, t[0], t[1]) for t in (mine, other)])
    left = copy_for_each(copy_for_each(sent, lines_of(0)), lines_of(1))

    held = [(mine, other)]
    for step in range(1, half + 1):
        if step == SETTLE:
            moved = list(held[-1])
            moved[CHAIN] = settle(moved[CHAIN], flops=FLOPS)
            held[-1] = tuple(moved)
        perm = ring + back if step < half else back
        held.append(tuple(lax.ppermute(t, ROWS, perm) for t in held[-1]))
    known = (plane_ref, core_ref, left, held)
    early = [(0, 0)] + [(i, None) for i in range(1, half)]
    totals = products(None, (0, 1), *known, early, [[1, 2], [3, 4], [5, 6], [7], [0]])
    late = [(half, 1)]
    outward = products(totals, (1,), *known, late, [[0]])[1]
    received = lax.ppermute(outward, "core", SWAP)
    total = products(totals, (0,), *known, late, [[0]])[0]
    inflated, sums = pl.pallas_call(
        functools.partial(square_kernel, columns),
        in_specs=[SMEM, SMEM, VMEM, VMEM],
        out_specs=[VMEM, VMEM],
        out_shape=[
            jax.ShapeDtypeStruct((2, width, width), jnp.float32),
            jax.ShapeDtypeStruct((2, width), jnp.float32),
        ],
        compiler_params=params(6),
    )(own, column_ref, total, received)
    sums = lax.all_gather(sums, "core", axis=0).sum(axis=0)
    parts = lax.all_to_all(
        jnp.broadcast_to(sums[None], (planes, *sums.shape)), "z", 0, 0, tiled=True
    )
    scale = float(planes * cores * width)
    out = pl.pallas_call(
        functools.partial(blend_kernel, scale, columns),
        in_specs=[SMEM, SMEM, VMEM, VMEM, VMEM],
        out_specs=VMEM,
        out_shape=jax.ShapeDtypeStruct((2, width, width), jnp.float32),
        compiler_params=params(6),
    )(own, column_ref, tiles, inflated, parts)
    return out[None]


def solution(mesh):
    physical = Mesh(mesh.devices.reshape(16, 2, 4, 4), (*ROWS, *COLS))
    tiled = P(ROWS, COLS, None, None)
    return jax.shard_map(
        on_device,
        mesh=physical,
        in_specs=(tiled, P(ROWS, COLS), P((*ROWS, *COLS), None)),
        out_specs=tiled,
        check_vma=False,
    )
```

```python
import functools

import jax
import jax.numpy as jnp
from jax import lax
from jax.experimental import pallas as pl
from jax.experimental.pallas import tpu as pltpu
from jax.sharding import Mesh, PartitionSpec as P

ROWS = ("z", "core")
COLS = ("y", "x")
SMEM = pl.BlockSpec(memory_space=pltpu.SMEM)
VMEM = pl.BlockSpec(memory_space=pltpu.VMEM)
ANY = pl.BlockSpec(memory_space=pl.ANY)
HBM = pl.BlockSpec(memory_space=pltpu.HBM)
MIB = 1024 * 1024
SWAP = [(0, 1), (1, 0)]
FLOPS = 26 * 10**9


def params(mib):
    return pltpu.CompilerParams(vmem_limit_bytes=mib * MIB)


def order_kernel(columns, own_ref, column_ref, tiles_ref, ordered_ref):
    for place in range(2):
        target = column_ref[0] + columns * place
        first = (own_ref[0] == target).astype(jnp.float32)
        second = (own_ref[1] == target).astype(jnp.float32)
        value = tiles_ref[0].astype(jnp.float32) * first + tiles_ref[1].astype(jnp.float32) * second
        ordered_ref[place] = value.astype(ordered_ref.dtype)


def settle_kernel(*refs):
    del refs


def fetch(plan, guard_ref, start):
    for copies, guard in plan:
        def go(copies=copies):
            for copy in copies:
                copy.start() if start else copy.wait()

        if guard is None:
            go()
        else:
            pl.when(guard_ref[0] == guard)(go)


def product_kernel(planes, rows, groups, plane_ref, core_ref, left_ref, *refs):
    count = 2 * len(planes)
    rights, refs = refs[:count], refs[count:]
    totals, (held, kept, sems) = refs[-3 - len(rows) : -3], refs[-3:]
    carried = len(refs) > 3 + len(rows)
    core = core_ref[0]
    breadth = left_ref.shape[0]
    columns = breadth * breadth
    plan = []
    for i, (distance, guard) in enumerate(planes):
        copies = []
        for j in range(2):
            inner = 2 * (plane_ref[0] + jnp.where(core == 0, -distance, distance))
            inner += jnp.where(core == 0, j, 1 - j)
            place = lax.rem(inner + 2 * columns, columns)
            y, x = place // breadth, lax.rem(place, breadth)
            outer, nested = jnp.where(core == 0, y, x), jnp.where(core == 0, x, y)
            for n, row in enumerate(rows):
                source = left_ref.at[outer, nested, row]
                copies.append(
                    pltpu.make_async_copy(source, held.at[2 * i + j, n], sems.at[2 * i + j, n])
                )
            copies.append(
                pltpu.make_async_copy(
                    rights[2 * i + j], kept.at[2 * i + j], sems.at[2 * i + j, len(rows)]
                )
            )
        plan.append((copies, guard))
    for group in groups:
        fetch([plan[i] for i in group], core_ref, True)
    if not carried:
        for total in totals:
            total[...] = jnp.zeros_like(total)
    width = held.shape[-1]
    for group in groups:
        fetch([plan[i] for i in group], core_ref, False)

        def add(group=group):
            tiles = [2 * i + j for i in group for j in range(2)]
            left = jnp.concatenate(
                [held[i].reshape(len(rows) * width, width) for i in tiles], axis=1
            )
            for column in range(2):
                right = jnp.concatenate([kept[i, column] for i in tiles], axis=0)
                product = jnp.dot(left, right, preferred_element_type=jnp.float32)
                for n, total in enumerate(totals):
                    total[column] += product[n * width : (n + 1) * width]

        guard = planes[group[0]][1]
        if guard is None:
            add()
        else:
            pl.when(core == guard)(add)


def products(totals, rows, plane, core, left, held, planes, groups):
    width = left.shape[-1]
    tiles = [tile for distance, _ in planes for tile in held[distance]]
    if len(planes) > 1:
        tiles = [pltpu.with_memory_space_constraint(tile, pltpu.HBM) for tile in tiles]
    given = [] if totals is None else [totals[row] for row in rows]
    kernel = functools.partial(product_kernel, planes, rows, groups)
    out = pl.pallas_call(
        kernel,
        in_specs=[SMEM, SMEM, HBM] + [HBM] * len(tiles) + [VMEM] * len(given),
        out_specs=[VMEM] * len(rows),
        out_shape=[jax.ShapeDtypeStruct((2, width, width), jnp.float32)] * len(rows),
        scratch_shapes=[
            pltpu.VMEM((len(tiles), len(rows), width, width), left.dtype),
            pltpu.VMEM((len(tiles), 2, width, width), left.dtype),
            pltpu.SemaphoreType.DMA((len(tiles), len(rows) + 1)),
        ],
        input_output_aliases={3 + len(tiles) + n: n for n in range(len(given))},
        compiler_params=params(10),
        cost_estimate=pl.CostEstimate(
            flops=4 * len(tiles) * len(rows) * width**3,
            bytes_accessed=4 * len(tiles) * (len(rows) + 2) * width**2,
            transcendentals=0,
        ),
    )(plane, core, left, *tiles, *given)
    return dict(zip(rows, out))


def square_kernel(columns, own_ref, column_ref, mine_ref, other_ref, inflated_ref, sums_ref):
    for place in range(2):
        target = column_ref[0] + columns * place
        kept = (own_ref[0] == target) | (own_ref[1] == target)
        value = mine_ref[place] + other_ref[place]
        value = jnp.where(kept, value * value, 0.0)
        inflated_ref[place] = value
        sums_ref[place : place + 1, :] = jnp.sum(value, axis=0, keepdims=True)


def blend_kernel(scale, columns, own_ref, column_ref, tiles_ref, inflated_ref, parts_ref, out_ref):
    totals = jnp.sum(parts_ref[...], axis=0)
    for slot in range(2):
        tile = tiles_ref[slot].astype(jnp.float32)
        for place in range(2):
            @pl.when(own_ref[slot] == column_ref[0] + columns * place)
            def _():
                normed = inflated_ref[place] * scale / totals[place : place + 1, :]
                out_ref[slot] = 0.5 * tile + 0.5 * normed

        @pl.when(own_ref[slot] < 0)
        def _():
            out_ref[slot] = jnp.zeros_like(tile)


def settle(value, after, flops):
    return pl.pallas_call(
        settle_kernel,
        in_specs=[ANY] * (1 + len(after)),
        out_specs=ANY,
        out_shape=jax.ShapeDtypeStruct(value.shape, value.dtype),
        input_output_aliases={0: 0},
        compiler_params=params(1),
        cost_estimate=pl.CostEstimate(flops=flops, bytes_accessed=0, transcendentals=0),
    )(value, *after)


def on_device(flow_tiles, tile_cols, pairs):
    width = flow_tiles.shape[3]
    planes, cores = lax.axis_size("z"), lax.axis_size("core")
    columns = lax.axis_size(COLS)
    plane, core, column = lax.axis_index("z"), lax.axis_index("core"), lax.axis_index(COLS)
    plane_ref, core_ref, column_ref = (
        i.astype(jnp.int32).reshape(1) for i in (plane, core, column)
    )
    own = pltpu.with_memory_space_constraint(tile_cols[0], pltpu.HBM)
    tiles = flow_tiles[0]
    mine = pl.pallas_call(
        functools.partial(order_kernel, columns),
        in_specs=[SMEM, SMEM, VMEM],
        out_specs=VMEM,
        out_shape=jax.ShapeDtypeStruct((2, width, width), tiles.dtype),
        compiler_params=params(4),
    )(own, column_ref, pltpu.with_memory_space_constraint(tiles, pltpu.HBM))
    other = lax.ppermute(mine, "core", SWAP)

    half = planes // 2
    ring = [(2 * z, 2 * ((z + 1) % planes)) for z in range(planes)]
    back = [(2 * z + 1, 2 * ((z - 1) % planes) + 1) for z in range(planes)]
    low = lax.rem(column - 2 * (plane - half + 1) + 2 * columns, 2 * columns)
    place = jnp.where((low < columns) == (core == 0), 0, 1)
    height, breadth = lax.axis_size("y"), lax.axis_size("x")
    assert height == breadth

    def lines_of(phase):
        lines = []
        for c in range(cores):
            for fixed in range(height):
                along_x = [breadth * fixed + i for i in range(breadth)]
                along_y = [breadth * i + fixed for i in range(height)]
                line = along_x if phase == c else along_y
                lines.append([columns * c + i for i in line])
        return lines

    def copy_for_each(value, lines):
        spread = jnp.broadcast_to(value[None], (len(lines[0]), *value.shape))
        return lax.all_to_all(
            spread, ("core", *COLS), 0, 0, axis_index_groups=lines, tiled=True
        )

    sent = jnp.stack([jnp.where(place == 0, t[0], t[1]) for t in (mine, other)])
    left = copy_for_each(copy_for_each(sent, lines_of(0)), lines_of(1))

    held = [(mine, other)]
    for step in range(1, half + 1):
        if step == half:
            known = (plane_ref, core_ref, left, held)
            early = [(i, 0) for i in range(half - 1)]
            totals = products(None, (0, 1), *known, early, [[0, 1], [2, 3], [4, 5], [6]])
            held[-1] = (held[-1][0], settle(held[-1][1], totals.values(), 0))
        elif step == half - 1:
            held[-1] = (held[-1][0], settle(held[-1][1], (), FLOPS))
        perm = ring + back if step < half else back
        held.append(tuple(lax.ppermute(t, ROWS, perm) for t in held[-1]))
    rest = [(i, 1) for i in range(1, half - 1)] + [(half - 1, None)]
    totals = products(totals, (0, 1), *known, rest, [[0, 1], [2, 3], [4, 5], [6]])
    late = [(half, 1)]
    outward = products(totals, (1,), *known, late, [[0]])[1]
    received = lax.ppermute(outward, "core", SWAP)
    total = products(totals, (0,), *known, late, [[0]])[0]
    inflated, sums = pl.pallas_call(
        functools.partial(square_kernel, columns),
        in_specs=[SMEM, SMEM, VMEM, VMEM],
        out_specs=[VMEM, VMEM],
        out_shape=[
            jax.ShapeDtypeStruct((2, width, width), jnp.float32),
            jax.ShapeDtypeStruct((2, width), jnp.float32),
        ],
        compiler_params=params(6),
    )(own, column_ref, total, received)
    sums = lax.all_gather(sums, "core", axis=0).sum(axis=0)
    parts = lax.all_to_all(
        jnp.broadcast_to(sums[None], (planes, *sums.shape)), "z", 0, 0, tiled=True
    )
    scale = float(planes * cores * width)
    out = pl.pallas_call(
        functools.partial(blend_kernel, scale, columns),
        in_specs=[SMEM, SMEM, VMEM, VMEM, VMEM],
        out_specs=VMEM,
        out_shape=jax.ShapeDtypeStruct((2, width, width), jnp.float32),
        compiler_params=params(6),
    )(own, column_ref, tiles, inflated, parts)
    return out[None]


def solution(mesh):
    physical = Mesh(mesh.devices.reshape(16, 2, 4, 4), (*ROWS, *COLS))
    tiled = P(ROWS, COLS, None, None)
    return jax.shard_map(
        on_device,
        mesh=physical,
        in_specs=(tiled, P(ROWS, COLS), P((*ROWS, *COLS), None)),
        out_specs=tiled,
        check_vma=False,
    )
```

```python
import functools

import jax
import jax.numpy as jnp
from jax import lax
from jax.experimental import pallas as pl
from jax.experimental.pallas import tpu as pltpu
from jax.sharding import Mesh, PartitionSpec as P

ROWS = ("z", "core")
COLS = ("y", "x")
SMEM = pl.BlockSpec(memory_space=pltpu.SMEM)
VMEM = pl.BlockSpec(memory_space=pltpu.VMEM)
ANY = pl.BlockSpec(memory_space=pl.ANY)
HBM = pl.BlockSpec(memory_space=pltpu.HBM)
MIB = 1024 * 1024
SWAP = [(0, 1), (1, 0)]
FLOPS = 26 * 10**9


def params(mib):
    return pltpu.CompilerParams(vmem_limit_bytes=mib * MIB)


def order_kernel(columns, own_ref, column_ref, tiles_ref, ordered_ref):
    for place in range(2):
        target = column_ref[0] + columns * place
        first = (own_ref[0] == target).astype(jnp.float32)
        second = (own_ref[1] == target).astype(jnp.float32)
        value = tiles_ref[0].astype(jnp.float32) * first + tiles_ref[1].astype(jnp.float32) * second
        ordered_ref[place] = value.astype(ordered_ref.dtype)


def settle_kernel(*refs):
    del refs


def fetch(plan, guard_ref, start):
    for copies, guard in plan:
        def go(copies=copies):
            for copy in copies:
                copy.start() if start else copy.wait()

        if guard is None:
            go()
        else:
            pl.when(guard_ref[0] == guard)(go)


def product_kernel(planes, rows, groups, plane_ref, core_ref, left_ref, *refs):
    count = 2 * len(planes)
    rights, refs = refs[:count], refs[count:]
    totals, (held, kept, sems) = refs[-3 - len(rows) : -3], refs[-3:]
    carried = len(refs) > 3 + len(rows)
    core = core_ref[0]
    breadth = left_ref.shape[0]
    columns = breadth * breadth
    plan = []
    for i, (distance, guard) in enumerate(planes):
        copies = []
        for j in range(2):
            inner = 2 * (plane_ref[0] + jnp.where(core == 0, -distance, distance))
            inner += jnp.where(core == 0, j, 1 - j)
            place = lax.rem(inner + 2 * columns, columns)
            y, x = place // breadth, lax.rem(place, breadth)
            outer, nested = jnp.where(core == 0, y, x), jnp.where(core == 0, x, y)
            for n, row in enumerate(rows):
                source = left_ref.at[outer, nested, row]
                copies.append(
                    pltpu.make_async_copy(source, held.at[2 * i + j, n], sems.at[2 * i + j, n])
                )
            copies.append(
                pltpu.make_async_copy(
                    rights[2 * i + j], kept.at[2 * i + j], sems.at[2 * i + j, len(rows)]
                )
            )
        plan.append((copies, guard))
    for group in groups:
        fetch([plan[i] for i in group], core_ref, True)
    if not carried:
        for total in totals:
            total[...] = jnp.zeros_like(total)
    width = held.shape[-1]
    for group in groups:
        fetch([plan[i] for i in group], core_ref, False)

        def add(group=group):
            tiles = [2 * i + j for i in group for j in range(2)]
            left = jnp.concatenate(
                [held[i].reshape(len(rows) * width, width) for i in tiles], axis=1
            )
            for column in range(2):
                right = jnp.concatenate([kept[i, column] for i in tiles], axis=0)
                product = jnp.dot(left, right, preferred_element_type=jnp.float32)
                for n, total in enumerate(totals):
                    total[column] += product[n * width : (n + 1) * width]

        guard = planes[group[0]][1]
        if guard is None:
            add()
        else:
            pl.when(core == guard)(add)


def products(totals, rows, plane, core, left, held, planes, groups):
    width = left.shape[-1]
    tiles = [tile for distance, _ in planes for tile in held[distance]]
    if len(planes) > 1:
        tiles = [pltpu.with_memory_space_constraint(tile, pltpu.HBM) for tile in tiles]
    given = [] if totals is None else [totals[row] for row in rows]
    kernel = functools.partial(product_kernel, planes, rows, groups)
    out = pl.pallas_call(
        kernel,
        in_specs=[SMEM, SMEM, HBM] + [HBM] * len(tiles) + [VMEM] * len(given),
        out_specs=[VMEM] * len(rows),
        out_shape=[jax.ShapeDtypeStruct((2, width, width), jnp.float32)] * len(rows),
        scratch_shapes=[
            pltpu.VMEM((len(tiles), len(rows), width, width), left.dtype),
            pltpu.VMEM((len(tiles), 2, width, width), left.dtype),
            pltpu.SemaphoreType.DMA((len(tiles), len(rows) + 1)),
        ],
        input_output_aliases={3 + len(tiles) + n: n for n in range(len(given))},
        compiler_params=params(10),
        cost_estimate=pl.CostEstimate(
            flops=4 * len(tiles) * len(rows) * width**3,
            bytes_accessed=4 * len(tiles) * (len(rows) + 2) * width**2,
            transcendentals=0,
        ),
    )(plane, core, left, *tiles, *given)
    return dict(zip(rows, out))


def square_kernel(columns, own_ref, column_ref, mine_ref, other_ref, inflated_ref, sums_ref):
    for place in range(2):
        target = column_ref[0] + columns * place
        kept = (own_ref[0] == target) | (own_ref[1] == target)
        value = mine_ref[place] + other_ref[place]
        value = jnp.where(kept, value * value, 0.0)
        inflated_ref[place] = value
        sums_ref[place : place + 1, :] = jnp.sum(value, axis=0, keepdims=True)


def blend_kernel(scale, columns, own_ref, column_ref, tiles_ref, inflated_ref, parts_ref, out_ref):
    totals = jnp.sum(parts_ref[...], axis=0)
    for slot in range(2):
        tile = tiles_ref[slot].astype(jnp.float32)
        for place in range(2):
            @pl.when(own_ref[slot] == column_ref[0] + columns * place)
            def _():
                normed = inflated_ref[place] * scale / totals[place : place + 1, :]
                out_ref[slot] = 0.5 * tile + 0.5 * normed

        @pl.when(own_ref[slot] < 0)
        def _():
            out_ref[slot] = jnp.zeros_like(tile)


def settle(value, after, flops):
    return pl.pallas_call(
        settle_kernel,
        in_specs=[ANY] * (1 + len(after)),
        out_specs=ANY,
        out_shape=jax.ShapeDtypeStruct(value.shape, value.dtype),
        input_output_aliases={0: 0},
        compiler_params=params(1),
        cost_estimate=pl.CostEstimate(flops=flops, bytes_accessed=0, transcendentals=0),
    )(value, *after)


def on_device(flow_tiles, tile_cols, pairs):
    width = flow_tiles.shape[3]
    planes, cores = lax.axis_size("z"), lax.axis_size("core")
    columns = lax.axis_size(COLS)
    plane, core, column = lax.axis_index("z"), lax.axis_index("core"), lax.axis_index(COLS)
    plane_ref, core_ref, column_ref = (
        i.astype(jnp.int32).reshape(1) for i in (plane, core, column)
    )
    own = pltpu.with_memory_space_constraint(tile_cols[0], pltpu.HBM)
    tiles = flow_tiles[0]
    mine = pl.pallas_call(
        functools.partial(order_kernel, columns),
        in_specs=[SMEM, SMEM, VMEM],
        out_specs=VMEM,
        out_shape=jax.ShapeDtypeStruct((2, width, width), tiles.dtype),
        compiler_params=params(4),
    )(own, column_ref, pltpu.with_memory_space_constraint(tiles, pltpu.HBM))
    other = lax.ppermute(mine, "core", SWAP)

    half = planes // 2
    ring = [(2 * z, 2 * ((z + 1) % planes)) for z in range(planes)]
    back = [(2 * z + 1, 2 * ((z - 1) % planes) + 1) for z in range(planes)]
    low = lax.rem(column - 2 * (plane - half + 1) + 2 * columns, 2 * columns)
    place = jnp.where((low < columns) == (core == 0), 0, 1)
    height, breadth = lax.axis_size("y"), lax.axis_size("x")
    assert height == breadth

    def lines_of(phase):
        lines = []
        for c in range(cores):
            for fixed in range(height):
                along_x = [breadth * fixed + i for i in range(breadth)]
                along_y = [breadth * i + fixed for i in range(height)]
                line = along_x if phase == c else along_y
                lines.append([columns * c + i for i in line])
        return lines

    def copy_for_each(value, lines):
        spread = jnp.broadcast_to(value[None], (len(lines[0]), *value.shape))
        return lax.all_to_all(
            spread, ("core", *COLS), 0, 0, axis_index_groups=lines, tiled=True
        )

    sent = jnp.stack([jnp.where(place == 0, t[0], t[1]) for t in (mine, other)])
    left = copy_for_each(copy_for_each(sent, lines_of(0)), lines_of(1))

    held = [(mine, other)]
    for step in range(1, half + 1):
        if step == half:
            known = (plane_ref, core_ref, left, held)
            early = [(i, 0) for i in range(half - 1)]
            totals = products(None, (0, 1), *known, early, [[0, 1], [2, 3], [4, 5], [6]])
            held[-1] = (held[-1][0], settle(held[-1][1], totals.values(), 0))
        elif step == half - 1:
            held[-1] = (held[-1][0], settle(held[-1][1], (), FLOPS))
        perm = ring + back if step < half else back
        held.append(tuple(lax.ppermute(t, ROWS, perm) for t in held[-1]))
    rest = [(i, 1) for i in range(1, half - 1)] + [(half - 1, None)]
    totals = products(totals, (0, 1), *known, rest, [[0, 1], [2, 3], [4, 5], [6]])
    late = [(half, 1)]
    outward = products(totals, (1,), *known, late, [[0]])[1]
    received = lax.ppermute(outward, "core", SWAP)
    total = products(totals, (0,), *known, late, [[0]])[0]
    inflated, sums = pl.pallas_call(
        functools.partial(square_kernel, columns),
        in_specs=[SMEM, SMEM, VMEM, VMEM],
        out_specs=[VMEM, VMEM],
        out_shape=[
            jax.ShapeDtypeStruct((2, width, width), jnp.float32),
            jax.ShapeDtypeStruct((2, width), jnp.float32),
        ],
        compiler_params=params(6),
    )(own, column_ref, total, received)
    parts = lax.all_to_all(
        jnp.broadcast_to(sums[None], (planes * cores, *sums.shape)), ROWS, 0, 0, tiled=True
    )
    scale = float(planes * cores * width)
    out = pl.pallas_call(
        functools.partial(blend_kernel, scale, columns),
        in_specs=[SMEM, SMEM, VMEM, VMEM, VMEM],
        out_specs=VMEM,
        out_shape=jax.ShapeDtypeStruct((2, width, width), jnp.float32),
        compiler_params=params(6),
    )(own, column_ref, tiles, inflated, parts)
    return out[None]


def solution(mesh):
    physical = Mesh(mesh.devices.reshape(16, 2, 4, 4), (*ROWS, *COLS))
    tiled = P(ROWS, COLS, None, None)
    return jax.shard_map(
        on_device,
        mesh=physical,
        in_specs=(tiled, P(ROWS, COLS), P((*ROWS, *COLS), None)),
        out_specs=tiled,
        check_vma=False,
    )
```

```python
import functools

import jax
import jax.numpy as jnp
from jax import lax
from jax.experimental import pallas as pl
from jax.experimental.pallas import tpu as pltpu
from jax.sharding import Mesh, PartitionSpec as P

ROWS = ("z", "core")
COLS = ("y", "x")
SMEM = pl.BlockSpec(memory_space=pltpu.SMEM)
VMEM = pl.BlockSpec(memory_space=pltpu.VMEM)
ANY = pl.BlockSpec(memory_space=pl.ANY)
HBM = pl.BlockSpec(memory_space=pltpu.HBM)
MIB = 1024 * 1024
SWAP = [(0, 1), (1, 0)]
FLOPS = 26 * 10**9


def params(mib):
    return pltpu.CompilerParams(vmem_limit_bytes=mib * MIB)


def order_kernel(columns, own_ref, column_ref, tiles_ref, ordered_ref):
    for place in range(2):
        target = column_ref[0] + columns * place
        first = (own_ref[0] == target).astype(jnp.float32)
        second = (own_ref[1] == target).astype(jnp.float32)
        value = tiles_ref[0].astype(jnp.float32) * first + tiles_ref[1].astype(jnp.float32) * second
        ordered_ref[place] = value.astype(ordered_ref.dtype)


def settle_kernel(*refs):
    del refs


def fetch(plan, guard_ref, start):
    for copies, guard in plan:
        def go(copies=copies):
            for copy in copies:
                copy.start() if start else copy.wait()

        if guard is None:
            go()
        else:
            pl.when(guard_ref[0] == guard)(go)


def product_kernel(planes, rows, groups, plane_ref, core_ref, left_ref, *refs):
    count = 2 * len(planes)
    rights, refs = refs[:count], refs[count:]
    totals, (held, kept, sems) = refs[-3 - len(rows) : -3], refs[-3:]
    carried = len(refs) > 3 + len(rows)
    core = core_ref[0]
    breadth = left_ref.shape[0]
    columns = breadth * breadth
    plan = []
    for i, (distance, guard) in enumerate(planes):
        copies = []
        for j in range(2):
            inner = 2 * (plane_ref[0] + jnp.where(core == 0, -distance, distance))
            inner += jnp.where(core == 0, j, 1 - j)
            place = lax.rem(inner + 2 * columns, columns)
            y, x = place // breadth, lax.rem(place, breadth)
            outer, nested = jnp.where(core == 0, y, x), jnp.where(core == 0, x, y)
            for n, row in enumerate(rows):
                source = left_ref.at[outer, nested, row]
                copies.append(
                    pltpu.make_async_copy(source, held.at[2 * i + j, n], sems.at[2 * i + j, n])
                )
            copies.append(
                pltpu.make_async_copy(
                    rights[2 * i + j], kept.at[2 * i + j], sems.at[2 * i + j, len(rows)]
                )
            )
        plan.append((copies, guard))
    for group in groups:
        fetch([plan[i] for i in group], core_ref, True)
    if not carried:
        for total in totals:
            total[...] = jnp.zeros_like(total)
    width = held.shape[-1]
    for group in groups:
        fetch([plan[i] for i in group], core_ref, False)

        def add(group=group):
            tiles = [2 * i + j for i in group for j in range(2)]
            left = jnp.concatenate(
                [held[i].reshape(len(rows) * width, width) for i in tiles], axis=1
            )
            for column in range(2):
                right = jnp.concatenate([kept[i, column] for i in tiles], axis=0)
                product = jnp.dot(left, right, preferred_element_type=jnp.float32)
                for n, total in enumerate(totals):
                    total[column] += product[n * width : (n + 1) * width]

        guard = planes[group[0]][1]
        if guard is None:
            add()
        else:
            pl.when(core == guard)(add)


def products(totals, rows, plane, core, left, held, planes, groups):
    width = left.shape[-1]
    tiles = [tile for distance, _ in planes for tile in held[distance]]
    if len(planes) > 1:
        tiles = [pltpu.with_memory_space_constraint(tile, pltpu.HBM) for tile in tiles]
    given = [] if totals is None else [totals[row] for row in rows]
    kernel = functools.partial(product_kernel, planes, rows, groups)
    out = pl.pallas_call(
        kernel,
        in_specs=[SMEM, SMEM, HBM] + [HBM] * len(tiles) + [VMEM] * len(given),
        out_specs=[VMEM] * len(rows),
        out_shape=[jax.ShapeDtypeStruct((2, width, width), jnp.float32)] * len(rows),
        scratch_shapes=[
            pltpu.VMEM((len(tiles), len(rows), width, width), left.dtype),
            pltpu.VMEM((len(tiles), 2, width, width), left.dtype),
            pltpu.SemaphoreType.DMA((len(tiles), len(rows) + 1)),
        ],
        input_output_aliases={3 + len(tiles) + n: n for n in range(len(given))},
        compiler_params=params(10),
        cost_estimate=pl.CostEstimate(
            flops=4 * len(tiles) * len(rows) * width**3,
            bytes_accessed=4 * len(tiles) * (len(rows) + 2) * width**2,
            transcendentals=0,
        ),
    )(plane, core, left, *tiles, *given)
    return dict(zip(rows, out))


def square_kernel(columns, own_ref, column_ref, mine_ref, other_ref, inflated_ref, sums_ref):
    for place in range(2):
        target = column_ref[0] + columns * place
        kept = (own_ref[0] == target) | (own_ref[1] == target)
        value = mine_ref[place] + other_ref[place]
        value = jnp.where(kept, value * value, 0.0)
        inflated_ref[place] = value
        sums_ref[place : place + 1, :] = jnp.sum(value, axis=0, keepdims=True)


def blend_kernel(scale, columns, own_ref, column_ref, tiles_ref, inflated_ref, parts_ref, out_ref):
    totals = jnp.sum(parts_ref[...], axis=0)
    for slot in range(2):
        tile = tiles_ref[slot].astype(jnp.float32)
        for place in range(2):
            @pl.when(own_ref[slot] == column_ref[0] + columns * place)
            def _():
                normed = inflated_ref[place] * scale / totals[place : place + 1, :]
                out_ref[slot] = 0.5 * tile + 0.5 * normed

        @pl.when(own_ref[slot] < 0)
        def _():
            out_ref[slot] = jnp.zeros_like(tile)


def settle(value, after, flops):
    return pl.pallas_call(
        settle_kernel,
        in_specs=[ANY] * (1 + len(after)),
        out_specs=ANY,
        out_shape=jax.ShapeDtypeStruct(value.shape, value.dtype),
        input_output_aliases={0: 0},
        compiler_params=params(1),
        cost_estimate=pl.CostEstimate(flops=flops, bytes_accessed=0, transcendentals=0),
    )(value, *after)


def on_device(flow_tiles, tile_cols, pairs):
    width = flow_tiles.shape[3]
    planes, cores = lax.axis_size("z"), lax.axis_size("core")
    columns = lax.axis_size(COLS)
    plane, core, column = lax.axis_index("z"), lax.axis_index("core"), lax.axis_index(COLS)
    plane_ref, core_ref, column_ref = (
        i.astype(jnp.int32).reshape(1) for i in (plane, core, column)
    )
    own = pltpu.with_memory_space_constraint(tile_cols[0], pltpu.HBM)
    tiles = flow_tiles[0]
    mine = pl.pallas_call(
        functools.partial(order_kernel, columns),
        in_specs=[SMEM, SMEM, VMEM],
        out_specs=VMEM,
        out_shape=jax.ShapeDtypeStruct((2, width, width), tiles.dtype),
        compiler_params=params(4),
    )(own, column_ref, pltpu.with_memory_space_constraint(tiles, pltpu.HBM))
    other = lax.ppermute(mine, "core", SWAP)

    half = planes // 2
    ring = [(2 * z, 2 * ((z + 1) % planes)) for z in range(planes)]
    back = [(2 * z + 1, 2 * ((z - 1) % planes) + 1) for z in range(planes)]
    low = lax.rem(column - 2 * (plane - half + 1) + 2 * columns, 2 * columns)
    place = jnp.where((low < columns) == (core == 0), 0, 1)
    height, breadth = lax.axis_size("y"), lax.axis_size("x")
    assert height == breadth

    def lines_of(phase):
        lines = []
        for c in range(cores):
            for fixed in range(height):
                along_x = [breadth * fixed + i for i in range(breadth)]
                along_y = [breadth * i + fixed for i in range(height)]
                line = along_x if phase == c else along_y
                lines.append([columns * c + i for i in line])
        return lines

    def copy_for_each(value, lines):
        spread = jnp.broadcast_to(value[None], (len(lines[0]), *value.shape))
        return lax.all_to_all(
            spread, ("core", *COLS), 0, 0, axis_index_groups=lines, tiled=True
        )

    sent = jnp.stack([jnp.where(place == 0, t[0], t[1]) for t in (mine, other)])
    left = copy_for_each(copy_for_each(sent, lines_of(0)), lines_of(1))

    held = [(mine, other)]
    for step in range(1, half + 1):
        if step == half:
            known = (plane_ref, core_ref, left, held)
            early = [(i, 0) for i in range(half - 1)]
            totals = products(None, (0, 1), *known, early, [[0, 1], [2, 3], [4, 5], [6]])
            held[-1] = (held[-1][0], settle(held[-1][1], totals.values(), 0))
        elif step == half - 1:
            held[-1] = (held[-1][0], settle(held[-1][1], (), FLOPS))
        perm = ring + back if step < half else back
        held.append(tuple(lax.ppermute(t, ROWS, perm) for t in held[-1]))
    rest = [(i, 1) for i in range(1, half - 1)] + [(half - 1, None)]
    totals = products(totals, (0, 1), *known, rest, [[0, 1], [2, 3], [4, 5], [6]])
    late = [(half, 1)]
    outward = products(totals, (1,), *known, late, [[0]])[1]
    received = lax.ppermute(outward, "core", SWAP)
    total = products(totals, (0,), *known, late, [[0]])[0]
    inflated, sums = pl.pallas_call(
        functools.partial(square_kernel, columns),
        in_specs=[SMEM, SMEM, VMEM, VMEM],
        out_specs=[VMEM, VMEM],
        out_shape=[
            jax.ShapeDtypeStruct((2, width, width), jnp.float32),
            jax.ShapeDtypeStruct((2, width), jnp.float32),
        ],
        compiler_params=params(6),
    )(own, column_ref, total, received)
    far = [(i + planes * cores // 2) % (planes * cores) for i in range(planes * cores)]
    parts = lax.all_to_all(
        jnp.broadcast_to(sums[None], (planes * cores, *sums.shape)),
        ROWS,
        0,
        0,
        axis_index_groups=[far],
        tiled=True,
    )
    scale = float(planes * cores * width)
    out = pl.pallas_call(
        functools.partial(blend_kernel, scale, columns),
        in_specs=[SMEM, SMEM, VMEM, VMEM, VMEM],
        out_specs=VMEM,
        out_shape=jax.ShapeDtypeStruct((2, width, width), jnp.float32),
        compiler_params=params(6),
    )(own, column_ref, tiles, inflated, parts)
    return out[None]


def solution(mesh):
    physical = Mesh(mesh.devices.reshape(16, 2, 4, 4), (*ROWS, *COLS))
    tiled = P(ROWS, COLS, None, None)
    return jax.shard_map(
        on_device,
        mesh=physical,
        in_specs=(tiled, P(ROWS, COLS), P((*ROWS, *COLS), None)),
        out_specs=tiled,
        check_vma=False,
    )
```

```python
import functools

import jax
import jax.numpy as jnp
from jax import lax
from jax.experimental import pallas as pl
from jax.experimental.pallas import tpu as pltpu
from jax.sharding import Mesh, PartitionSpec as P

ROWS = ("z", "core")
COLS = ("y", "x")
SMEM = pl.BlockSpec(memory_space=pltpu.SMEM)
VMEM = pl.BlockSpec(memory_space=pltpu.VMEM)
ANY = pl.BlockSpec(memory_space=pl.ANY)
HBM = pl.BlockSpec(memory_space=pltpu.HBM)
MIB = 1024 * 1024
SWAP = [(0, 1), (1, 0)]
FLOPS = 26 * 10**9


def params(mib):
    return pltpu.CompilerParams(vmem_limit_bytes=mib * MIB)


def order_kernel(columns, own_ref, column_ref, tiles_ref, ordered_ref):
    for place in range(2):
        target = column_ref[0] + columns * place
        first = (own_ref[0] == target).astype(jnp.float32)
        second = (own_ref[1] == target).astype(jnp.float32)
        value = tiles_ref[0].astype(jnp.float32) * first + tiles_ref[1].astype(jnp.float32) * second
        ordered_ref[place] = value.astype(ordered_ref.dtype)


def settle_kernel(*refs):
    del refs


def fetch(plan, guard_ref, start):
    for copies, guard in plan:
        def go(copies=copies):
            for copy in copies:
                copy.start() if start else copy.wait()

        if guard is None:
            go()
        else:
            pl.when(guard_ref[0] == guard)(go)


def product_kernel(planes, rows, groups, plane_ref, core_ref, left_ref, *refs):
    count = 2 * len(planes)
    rights, refs = refs[:count], refs[count:]
    totals, (held, kept, sems) = refs[-3 - len(rows) : -3], refs[-3:]
    carried = len(refs) > 3 + len(rows)
    core = core_ref[0]
    breadth = left_ref.shape[0]
    columns = breadth * breadth
    plan = []
    for i, (distance, guard) in enumerate(planes):
        copies = []
        for j in range(2):
            inner = 2 * (plane_ref[0] + jnp.where(core == 0, -distance, distance))
            inner += jnp.where(core == 0, j, 1 - j)
            place = lax.rem(inner + 2 * columns, columns)
            y, x = place // breadth, lax.rem(place, breadth)
            outer, nested = jnp.where(core == 0, y, x), jnp.where(core == 0, x, y)
            for n, row in enumerate(rows):
                source = left_ref.at[outer, nested, row]
                copies.append(
                    pltpu.make_async_copy(source, held.at[2 * i + j, n], sems.at[2 * i + j, n])
                )
            copies.append(
                pltpu.make_async_copy(
                    rights[2 * i + j], kept.at[2 * i + j], sems.at[2 * i + j, len(rows)]
                )
            )
        plan.append((copies, guard))
    for group in groups:
        fetch([plan[i] for i in group], core_ref, True)
    if not carried:
        for total in totals:
            total[...] = jnp.zeros_like(total)
    width = held.shape[-1]
    for group in groups:
        fetch([plan[i] for i in group], core_ref, False)

        def add(group=group):
            tiles = [2 * i + j for i in group for j in range(2)]
            left = jnp.concatenate(
                [held[i].reshape(len(rows) * width, width) for i in tiles], axis=1
            )
            for column in range(2):
                right = jnp.concatenate([kept[i, column] for i in tiles], axis=0)
                product = jnp.dot(left, right, preferred_element_type=jnp.float32)
                for n, total in enumerate(totals):
                    total[column] += product[n * width : (n + 1) * width]

        guard = planes[group[0]][1]
        if guard is None:
            add()
        else:
            pl.when(core == guard)(add)


def products(totals, rows, plane, core, left, held, planes, groups):
    width = left.shape[-1]
    tiles = [tile for distance, _ in planes for tile in held[distance]]
    if len(planes) > 1:
        tiles = [pltpu.with_memory_space_constraint(tile, pltpu.HBM) for tile in tiles]
    given = [] if totals is None else [totals[row] for row in rows]
    kernel = functools.partial(product_kernel, planes, rows, groups)
    out = pl.pallas_call(
        kernel,
        in_specs=[SMEM, SMEM, HBM] + [HBM] * len(tiles) + [VMEM] * len(given),
        out_specs=[VMEM] * len(rows),
        out_shape=[jax.ShapeDtypeStruct((2, width, width), jnp.float32)] * len(rows),
        scratch_shapes=[
            pltpu.VMEM((len(tiles), len(rows), width, width), left.dtype),
            pltpu.VMEM((len(tiles), 2, width, width), left.dtype),
            pltpu.SemaphoreType.DMA((len(tiles), len(rows) + 1)),
        ],
        input_output_aliases={3 + len(tiles) + n: n for n in range(len(given))},
        compiler_params=params(10),
        cost_estimate=pl.CostEstimate(
            flops=4 * len(tiles) * len(rows) * width**3,
            bytes_accessed=4 * len(tiles) * (len(rows) + 2) * width**2,
            transcendentals=0,
        ),
    )(plane, core, left, *tiles, *given)
    return dict(zip(rows, out))


def square_kernel(columns, own_ref, column_ref, mine_ref, other_ref, inflated_ref, sums_ref):
    for place in range(2):
        target = column_ref[0] + columns * place
        kept = (own_ref[0] == target) | (own_ref[1] == target)
        value = mine_ref[place] + other_ref[place]
        value = jnp.where(kept, value * value, 0.0)
        inflated_ref[place] = value
        sums_ref[place : place + 1, :] = jnp.sum(value, axis=0, keepdims=True)


def blend_kernel(scale, columns, own_ref, column_ref, tiles_ref, inflated_ref, parts_ref, out_ref):
    totals = jnp.sum(parts_ref[...], axis=0)
    for slot in range(2):
        tile = tiles_ref[slot].astype(jnp.float32)
        for place in range(2):
            @pl.when(own_ref[slot] == column_ref[0] + columns * place)
            def _():
                normed = inflated_ref[place] * scale / totals[place : place + 1, :]
                out_ref[slot] = 0.5 * tile + 0.5 * normed

        @pl.when(own_ref[slot] < 0)
        def _():
            out_ref[slot] = jnp.zeros_like(tile)


def settle(value, after, flops):
    return pl.pallas_call(
        settle_kernel,
        in_specs=[ANY] * (1 + len(after)),
        out_specs=ANY,
        out_shape=jax.ShapeDtypeStruct(value.shape, value.dtype),
        input_output_aliases={0: 0},
        compiler_params=params(1),
        cost_estimate=pl.CostEstimate(flops=flops, bytes_accessed=0, transcendentals=0),
    )(value, *after)


def on_device(flow_tiles, tile_cols, pairs):
    width = flow_tiles.shape[3]
    planes, cores = lax.axis_size("z"), lax.axis_size("core")
    columns = lax.axis_size(COLS)
    plane, core, column = lax.axis_index("z"), lax.axis_index("core"), lax.axis_index(COLS)
    plane_ref, core_ref, column_ref = (
        i.astype(jnp.int32).reshape(1) for i in (plane, core, column)
    )
    own = pltpu.with_memory_space_constraint(tile_cols[0], pltpu.HBM)
    tiles = flow_tiles[0]
    mine = pl.pallas_call(
        functools.partial(order_kernel, columns),
        in_specs=[SMEM, SMEM, VMEM],
        out_specs=VMEM,
        out_shape=jax.ShapeDtypeStruct((2, width, width), tiles.dtype),
        compiler_params=params(4),
    )(own, column_ref, pltpu.with_memory_space_constraint(tiles, pltpu.HBM))
    other = lax.ppermute(mine, "core", SWAP)

    half = planes // 2
    ring = [(2 * z, 2 * ((z + 1) % planes)) for z in range(planes)]
    back = [(2 * z + 1, 2 * ((z - 1) % planes) + 1) for z in range(planes)]
    low = lax.rem(column - 2 * (plane - half + 1) + 2 * columns, 2 * columns)
    place = jnp.where((low < columns) == (core == 0), 0, 1)
    height, breadth = lax.axis_size("y"), lax.axis_size("x")
    assert height == breadth

    def lines_of(phase):
        lines = []
        for c in range(cores):
            for fixed in range(height):
                along_x = [breadth * fixed + i for i in range(breadth)]
                along_y = [breadth * i + fixed for i in range(height)]
                line = along_x if phase == c else along_y
                lines.append([columns * c + i for i in line])
        return lines

    def copy_for_each(value, lines):
        spread = jnp.broadcast_to(value[None], (len(lines[0]), *value.shape))
        return lax.all_to_all(
            spread, ("core", *COLS), 0, 0, axis_index_groups=lines, tiled=True
        )

    sent = jnp.stack([jnp.where(place == 0, t[0], t[1]) for t in (mine, other)])
    left = copy_for_each(copy_for_each(sent, lines_of(0)), lines_of(1))

    held = [(mine, other)]
    for step in range(1, half + 1):
        if step == half:
            known = (plane_ref, core_ref, left, held)
            early = [(i, 0) for i in range(half - 1)]
            totals = products(None, (0, 1), *known, early, [[0, 1], [2, 3], [4, 5], [6]])
            held[-1] = (held[-1][0], settle(held[-1][1], totals.values(), 0))
        elif step == half - 1:
            held[-1] = (held[-1][0], settle(held[-1][1], (), FLOPS))
        perm = ring + back if step < half else back
        held.append(tuple(lax.ppermute(t, ROWS, perm) for t in held[-1]))
    rest = [(i, 1) for i in range(1, half - 1)] + [(half - 1, None)]
    totals = products(totals, (0, 1), *known, rest, [[0, 1], [2, 3], [4, 5], [6]])
    late = [(half, 1)]
    outward = products(totals, (1,), *known, late, [[0]])[1]
    received = lax.ppermute(outward, "core", SWAP)
    total = products(totals, (0,), *known, late, [[0]])[0]
    inflated, sums = pl.pallas_call(
        functools.partial(square_kernel, columns),
        in_specs=[SMEM, SMEM, VMEM, VMEM],
        out_specs=[VMEM, VMEM],
        out_shape=[
            jax.ShapeDtypeStruct((2, width, width), jnp.float32),
            jax.ShapeDtypeStruct((2, width), jnp.float32),
        ],
        compiler_params=params(6),
    )(own, column_ref, total, received)
    order = sorted(range(planes), key=lambda z: min(z, planes - z))
    far = [cores * z + c for z in order[-1:] + order[:-1] for c in range(cores)]
    parts = lax.all_to_all(
        jnp.broadcast_to(sums[None], (planes * cores, *sums.shape)),
        ROWS,
        0,
        0,
        axis_index_groups=[far],
        tiled=True,
    )
    scale = float(planes * cores * width)
    out = pl.pallas_call(
        functools.partial(blend_kernel, scale, columns),
        in_specs=[SMEM, SMEM, VMEM, VMEM, VMEM],
        out_specs=VMEM,
        out_shape=jax.ShapeDtypeStruct((2, width, width), jnp.float32),
        compiler_params=params(6),
    )(own, column_ref, tiles, inflated, parts)
    return out[None]


def solution(mesh):
    physical = Mesh(mesh.devices.reshape(16, 2, 4, 4), (*ROWS, *COLS))
    tiled = P(ROWS, COLS, None, None)
    return jax.shard_map(
        on_device,
        mesh=physical,
        in_specs=(tiled, P(ROWS, COLS), P((*ROWS, *COLS), None)),
        out_specs=tiled,
        check_vma=False,
    )
```

```python
import functools

import jax
import jax.numpy as jnp
from jax import lax
from jax.experimental import pallas as pl
from jax.experimental.pallas import tpu as pltpu
from jax.sharding import Mesh, PartitionSpec as P

ROWS = ("z", "core")
COLS = ("y", "x")
SMEM = pl.BlockSpec(memory_space=pltpu.SMEM)
VMEM = pl.BlockSpec(memory_space=pltpu.VMEM)
ANY = pl.BlockSpec(memory_space=pl.ANY)
HBM = pl.BlockSpec(memory_space=pltpu.HBM)
MIB = 1024 * 1024
SWAP = [(0, 1), (1, 0)]
FLOPS = 26 * 10**9


def params(mib):
    return pltpu.CompilerParams(vmem_limit_bytes=mib * MIB)


def order_kernel(columns, own_ref, column_ref, tiles_ref, ordered_ref):
    for place in range(2):
        target = column_ref[0] + columns * place
        first = (own_ref[0] == target).astype(jnp.float32)
        second = (own_ref[1] == target).astype(jnp.float32)
        value = tiles_ref[0].astype(jnp.float32) * first + tiles_ref[1].astype(jnp.float32) * second
        ordered_ref[place] = value.astype(ordered_ref.dtype)


def settle_kernel(*refs):
    del refs


def fetch(plan, guard_ref, start):
    for copies, guard in plan:
        def go(copies=copies):
            for copy in copies:
                copy.start() if start else copy.wait()

        if guard is None:
            go()
        else:
            pl.when(guard_ref[0] == guard)(go)


def product_kernel(planes, rows, groups, plane_ref, core_ref, left_ref, *refs):
    count = 2 * len(planes)
    rights, refs = refs[:count], refs[count:]
    totals, (held, kept, sems) = refs[-3 - len(rows) : -3], refs[-3:]
    carried = len(refs) > 3 + len(rows)
    core = core_ref[0]
    breadth = left_ref.shape[0]
    columns = breadth * breadth
    plan = []
    for i, (distance, guard) in enumerate(planes):
        copies = []
        for j in range(2):
            inner = 2 * (plane_ref[0] + jnp.where(core == 0, -distance, distance))
            inner += jnp.where(core == 0, j, 1 - j)
            place = lax.rem(inner + 2 * columns, columns)
            y, x = place // breadth, lax.rem(place, breadth)
            outer, nested = jnp.where(core == 0, y, x), jnp.where(core == 0, x, y)
            for n, row in enumerate(rows):
                source = left_ref.at[outer, nested, row]
                copies.append(
                    pltpu.make_async_copy(source, held.at[2 * i + j, n], sems.at[2 * i + j, n])
                )
            copies.append(
                pltpu.make_async_copy(
                    rights[2 * i + j], kept.at[2 * i + j], sems.at[2 * i + j, len(rows)]
                )
            )
        plan.append((copies, guard))
    for group in groups:
        fetch([plan[i] for i in group], core_ref, True)
    if not carried:
        for total in totals:
            total[...] = jnp.zeros_like(total)
    width = held.shape[-1]
    for group in groups:
        fetch([plan[i] for i in group], core_ref, False)

        def add(group=group):
            tiles = [2 * i + j for i in group for j in range(2)]
            left = jnp.concatenate(
                [held[i].reshape(len(rows) * width, width) for i in tiles], axis=1
            )
            for column in range(2):
                right = jnp.concatenate([kept[i, column] for i in tiles], axis=0)
                product = jnp.dot(left, right, preferred_element_type=jnp.float32)
                for n, total in enumerate(totals):
                    total[column] += product[n * width : (n + 1) * width]

        guard = planes[group[0]][1]
        if guard is None:
            add()
        else:
            pl.when(core == guard)(add)


def products(totals, rows, plane, core, left, held, planes, groups):
    width = left.shape[-1]
    tiles = [tile for distance, _ in planes for tile in held[distance]]
    if len(planes) > 1:
        tiles = [pltpu.with_memory_space_constraint(tile, pltpu.HBM) for tile in tiles]
    given = [] if totals is None else [totals[row] for row in rows]
    kernel = functools.partial(product_kernel, planes, rows, groups)
    out = pl.pallas_call(
        kernel,
        in_specs=[SMEM, SMEM, HBM] + [HBM] * len(tiles) + [VMEM] * len(given),
        out_specs=[VMEM] * len(rows),
        out_shape=[jax.ShapeDtypeStruct((2, width, width), jnp.float32)] * len(rows),
        scratch_shapes=[
            pltpu.VMEM((len(tiles), len(rows), width, width), left.dtype),
            pltpu.VMEM((len(tiles), 2, width, width), left.dtype),
            pltpu.SemaphoreType.DMA((len(tiles), len(rows) + 1)),
        ],
        input_output_aliases={3 + len(tiles) + n: n for n in range(len(given))},
        compiler_params=params(10),
        cost_estimate=pl.CostEstimate(
            flops=4 * len(tiles) * len(rows) * width**3,
            bytes_accessed=4 * len(tiles) * (len(rows) + 2) * width**2,
            transcendentals=0,
        ),
    )(plane, core, left, *tiles, *given)
    return dict(zip(rows, out))


def square_kernel(columns, own_ref, column_ref, mine_ref, other_ref, inflated_ref, sums_ref):
    for place in range(2):
        target = column_ref[0] + columns * place
        kept = (own_ref[0] == target) | (own_ref[1] == target)
        value = mine_ref[place] + other_ref[place]
        value = jnp.where(kept, value * value, 0.0)
        inflated_ref[place] = value
        sums_ref[place : place + 1, :] = jnp.sum(value, axis=0, keepdims=True)


def blend_kernel(scale, columns, own_ref, column_ref, tiles_ref, inflated_ref, parts_ref, out_ref):
    totals = jnp.sum(parts_ref[...], axis=0)
    for slot in range(2):
        tile = tiles_ref[slot].astype(jnp.float32)
        for place in range(2):
            @pl.when(own_ref[slot] == column_ref[0] + columns * place)
            def _():
                normed = inflated_ref[place] * scale / totals[place : place + 1, :]
                out_ref[slot] = 0.5 * tile + 0.5 * normed

        @pl.when(own_ref[slot] < 0)
        def _():
            out_ref[slot] = jnp.zeros_like(tile)


def settle(value, after, flops):
    return pl.pallas_call(
        settle_kernel,
        in_specs=[ANY] * (1 + len(after)),
        out_specs=ANY,
        out_shape=jax.ShapeDtypeStruct(value.shape, value.dtype),
        input_output_aliases={0: 0},
        compiler_params=params(1),
        cost_estimate=pl.CostEstimate(flops=flops, bytes_accessed=0, transcendentals=0),
    )(value, *after)


def on_device(flow_tiles, tile_cols, pairs):
    width = flow_tiles.shape[3]
    planes, cores = lax.axis_size("z"), lax.axis_size("core")
    columns = lax.axis_size(COLS)
    plane, core, column = lax.axis_index("z"), lax.axis_index("core"), lax.axis_index(COLS)
    plane_ref, core_ref, column_ref = (
        i.astype(jnp.int32).reshape(1) for i in (plane, core, column)
    )
    own = pltpu.with_memory_space_constraint(tile_cols[0], pltpu.HBM)
    tiles = flow_tiles[0]
    mine = pl.pallas_call(
        functools.partial(order_kernel, columns),
        in_specs=[SMEM, SMEM, VMEM],
        out_specs=VMEM,
        out_shape=jax.ShapeDtypeStruct((2, width, width), tiles.dtype),
        compiler_params=params(4),
    )(own, column_ref, pltpu.with_memory_space_constraint(tiles, pltpu.HBM))
    other = lax.ppermute(mine, "core", SWAP)

    half = planes // 2
    ring = [(2 * z, 2 * ((z + 1) % planes)) for z in range(planes)]
    back = [(2 * z + 1, 2 * ((z - 1) % planes) + 1) for z in range(planes)]
    low = lax.rem(column - 2 * (plane - half + 1) + 2 * columns, 2 * columns)
    place = jnp.where((low < columns) == (core == 0), 0, 1)
    height, breadth = lax.axis_size("y"), lax.axis_size("x")
    assert height == breadth

    def lines_of(phase):
        lines = []
        for c in range(cores):
            for fixed in range(height):
                along_x = [breadth * fixed + i for i in range(breadth)]
                along_y = [breadth * i + fixed for i in range(height)]
                line = along_x if phase == c else along_y
                lines.append([columns * c + i for i in line])
        return lines

    def copy_for_each(value, lines):
        spread = jnp.broadcast_to(value[None], (len(lines[0]), *value.shape))
        return lax.all_to_all(
            spread, ("core", *COLS), 0, 0, axis_index_groups=lines, tiled=True
        )

    sent = jnp.stack([jnp.where(place == 0, t[0], t[1]) for t in (mine, other)])
    left = copy_for_each(copy_for_each(sent, lines_of(0)), lines_of(1))

    held = [(mine, other)]
    for step in range(1, half + 1):
        if step == half:
            known = (plane_ref, core_ref, left, held)
            early = [(i, 0) for i in range(half - 1)]
            totals = products(None, (0, 1), *known, early, [[0, 1], [2, 3], [4, 5], [6]])
            held[-1] = (held[-1][0], settle(held[-1][1], totals.values(), 0))
        elif step == half - 1:
            held[-1] = (held[-1][0], settle(held[-1][1], (), FLOPS))
        perm = ring + back if step < half else back
        held.append(tuple(lax.ppermute(t, ROWS, perm) for t in held[-1]))
    rest = [(i, 1) for i in range(1, half - 1)] + [(half - 1, None)]
    totals = products(totals, (0, 1), *known, rest, [[0, 1], [2, 3], [4, 5], [6]])
    late = [(half, 1)]
    outward = products(totals, (1,), *known, late, [[0]])[1]
    received = lax.ppermute(outward, "core", SWAP)
    total = products(totals, (0,), *known, late, [[0]])[0]
    inflated, sums = pl.pallas_call(
        functools.partial(square_kernel, columns),
        in_specs=[SMEM, SMEM, VMEM, VMEM],
        out_specs=[VMEM, VMEM],
        out_shape=[
            jax.ShapeDtypeStruct((2, width, width), jnp.float32),
            jax.ShapeDtypeStruct((2, width), jnp.float32),
        ],
        compiler_params=params(6),
    )(own, column_ref, total, received)
    sums = lax.all_gather(sums, "core", axis=0).sum(axis=0)
    far = [(z + half) % planes for z in range(planes)]
    parts = lax.all_to_all(
        jnp.broadcast_to(sums[None], (planes, *sums.shape)),
        "z",
        0,
        0,
        axis_index_groups=[far],
        tiled=True,
    )
    scale = float(planes * cores * width)
    out = pl.pallas_call(
        functools.partial(blend_kernel, scale, columns),
        in_specs=[SMEM, SMEM, VMEM, VMEM, VMEM],
        out_specs=VMEM,
        out_shape=jax.ShapeDtypeStruct((2, width, width), jnp.float32),
        compiler_params=params(6),
    )(own, column_ref, tiles, inflated, parts)
    return out[None]


def solution(mesh):
    physical = Mesh(mesh.devices.reshape(16, 2, 4, 4), (*ROWS, *COLS))
    tiled = P(ROWS, COLS, None, None)
    return jax.shard_map(
        on_device,
        mesh=physical,
        in_specs=(tiled, P(ROWS, COLS), P((*ROWS, *COLS), None)),
        out_specs=tiled,
        check_vma=False,
    )
```

```python
import functools

import jax
import jax.numpy as jnp
from jax import lax
from jax.experimental import pallas as pl
from jax.experimental.pallas import tpu as pltpu
from jax.sharding import Mesh, PartitionSpec as P

ROWS = ("z", "core")
COLS = ("y", "x")
SMEM = pl.BlockSpec(memory_space=pltpu.SMEM)
VMEM = pl.BlockSpec(memory_space=pltpu.VMEM)
ANY = pl.BlockSpec(memory_space=pl.ANY)
HBM = pl.BlockSpec(memory_space=pltpu.HBM)
MIB = 1024 * 1024
SWAP = [(0, 1), (1, 0)]
FLOPS = 26 * 10**9


def params(mib):
    return pltpu.CompilerParams(vmem_limit_bytes=mib * MIB)


def order_kernel(columns, own_ref, column_ref, tiles_ref, ordered_ref):
    for place in range(2):
        target = column_ref[0] + columns * place
        first = (own_ref[0] == target).astype(jnp.float32)
        second = (own_ref[1] == target).astype(jnp.float32)
        value = tiles_ref[0].astype(jnp.float32) * first + tiles_ref[1].astype(jnp.float32) * second
        ordered_ref[place] = value.astype(ordered_ref.dtype)


def settle_kernel(*refs):
    del refs


def fetch(plan, guard_ref, start):
    for copies, guard in plan:
        def go(copies=copies):
            for copy in copies:
                copy.start() if start else copy.wait()

        if guard is None:
            go()
        else:
            pl.when(guard_ref[0] == guard)(go)


def product_kernel(planes, rows, groups, plane_ref, core_ref, left_ref, *refs):
    count = 2 * len(planes)
    rights, refs = refs[:count], refs[count:]
    totals, (held, kept, sems) = refs[-3 - len(rows) : -3], refs[-3:]
    carried = len(refs) > 3 + len(rows)
    core = core_ref[0]
    breadth = left_ref.shape[0]
    columns = breadth * breadth
    plan = []
    for i, (distance, guard) in enumerate(planes):
        copies = []
        for j in range(2):
            inner = 2 * (plane_ref[0] + jnp.where(core == 0, -distance, distance))
            inner += jnp.where(core == 0, j, 1 - j)
            place = lax.rem(inner + 2 * columns, columns)
            y, x = place // breadth, lax.rem(place, breadth)
            outer, nested = jnp.where(core == 0, y, x), jnp.where(core == 0, x, y)
            for n, row in enumerate(rows):
                source = left_ref.at[outer, nested, row]
                copies.append(
                    pltpu.make_async_copy(source, held.at[2 * i + j, n], sems.at[2 * i + j, n])
                )
            copies.append(
                pltpu.make_async_copy(
                    rights[2 * i + j], kept.at[2 * i + j], sems.at[2 * i + j, len(rows)]
                )
            )
        plan.append((copies, guard))
    for group in groups:
        fetch([plan[i] for i in group], core_ref, True)
    if len(planes) > 1:
        @pl.when(core == int(carried))
        def _():
            for total in totals:
                total[...] = jnp.zeros_like(total)

    width = held.shape[-1]
    for group in groups:
        fetch([plan[i] for i in group], core_ref, False)

        def add(group=group):
            tiles = [2 * i + j for i in group for j in range(2)]
            left = jnp.concatenate(
                [held[i].reshape(len(rows) * width, width) for i in tiles], axis=1
            )
            for column in range(2):
                right = jnp.concatenate([kept[i, column] for i in tiles], axis=0)
                product = jnp.dot(left, right, preferred_element_type=jnp.float32)
                for n, total in enumerate(totals):
                    total[column] += product[n * width : (n + 1) * width]

        guard = planes[group[0]][1]
        if guard is None:
            add()
        else:
            pl.when(core == guard)(add)


def products(totals, rows, plane, core, left, held, planes, groups):
    width = left.shape[-1]
    tiles = [tile for distance, _ in planes for tile in held[distance]]
    if len(planes) > 1:
        tiles = [pltpu.with_memory_space_constraint(tile, pltpu.HBM) for tile in tiles]
    given = [] if totals is None else [totals[row] for row in rows]
    kernel = functools.partial(product_kernel, planes, rows, groups)
    out = pl.pallas_call(
        kernel,
        in_specs=[SMEM, SMEM, HBM] + [HBM] * len(tiles) + [VMEM] * len(given),
        out_specs=[VMEM] * len(rows),
        out_shape=[jax.ShapeDtypeStruct((2, width, width), jnp.float32)] * len(rows),
        scratch_shapes=[
            pltpu.VMEM((len(tiles), len(rows), width, width), left.dtype),
            pltpu.VMEM((len(tiles), 2, width, width), left.dtype),
            pltpu.SemaphoreType.DMA((len(tiles), len(rows) + 1)),
        ],
        input_output_aliases={3 + len(tiles) + n: n for n in range(len(given))},
        compiler_params=params(10),
        cost_estimate=pl.CostEstimate(
            flops=4 * len(tiles) * len(rows) * width**3,
            bytes_accessed=4 * len(tiles) * (len(rows) + 2) * width**2,
            transcendentals=0,
        ),
    )(plane, core, left, *tiles, *given)
    return dict(zip(rows, out))


def square_kernel(columns, own_ref, column_ref, mine_ref, other_ref, inflated_ref, sums_ref):
    for place in range(2):
        target = column_ref[0] + columns * place
        kept = (own_ref[0] == target) | (own_ref[1] == target)
        value = mine_ref[place] + other_ref[place]
        value = jnp.where(kept, value * value, 0.0)
        inflated_ref[place] = value
        sums_ref[place : place + 1, :] = jnp.sum(value, axis=0, keepdims=True)


def blend_kernel(scale, columns, own_ref, column_ref, tiles_ref, inflated_ref, parts_ref, out_ref):
    factors = 0.5 * scale / jnp.sum(parts_ref[...], axis=0)
    for slot in range(2):
        tile = tiles_ref[slot].astype(jnp.float32)
        for place in range(2):
            @pl.when(own_ref[slot] == column_ref[0] + columns * place)
            def _():
                out_ref[slot] = 0.5 * tile + inflated_ref[place] * factors[place : place + 1, :]

        @pl.when(own_ref[slot] < 0)
        def _():
            out_ref[slot] = jnp.zeros_like(tile)


def settle(value, after, flops):
    return pl.pallas_call(
        settle_kernel,
        in_specs=[ANY] * (1 + len(after)),
        out_specs=ANY,
        out_shape=jax.ShapeDtypeStruct(value.shape, value.dtype),
        input_output_aliases={0: 0},
        compiler_params=params(1),
        cost_estimate=pl.CostEstimate(flops=flops, bytes_accessed=0, transcendentals=0),
    )(value, *after)


def on_device(flow_tiles, tile_cols, pairs):
    width = flow_tiles.shape[3]
    planes, cores = lax.axis_size("z"), lax.axis_size("core")
    columns = lax.axis_size(COLS)
    plane, core, column = lax.axis_index("z"), lax.axis_index("core"), lax.axis_index(COLS)
    plane_ref, core_ref, column_ref = (
        i.astype(jnp.int32).reshape(1) for i in (plane, core, column)
    )
    own = pltpu.with_memory_space_constraint(tile_cols[0], pltpu.HBM)
    tiles = flow_tiles[0]
    mine = pl.pallas_call(
        functools.partial(order_kernel, columns),
        in_specs=[SMEM, SMEM, VMEM],
        out_specs=VMEM,
        out_shape=jax.ShapeDtypeStruct((2, width, width), tiles.dtype),
        compiler_params=params(4),
    )(own, column_ref, pltpu.with_memory_space_constraint(tiles, pltpu.HBM))
    other = lax.ppermute(mine, "core", SWAP)

    half = planes // 2
    ring = [(2 * z, 2 * ((z + 1) % planes)) for z in range(planes)]
    back = [(2 * z + 1, 2 * ((z - 1) % planes) + 1) for z in range(planes)]
    low = lax.rem(column - 2 * (plane - half + 1) + 2 * columns, 2 * columns)
    place = jnp.where((low < columns) == (core == 0), 0, 1)
    height, breadth = lax.axis_size("y"), lax.axis_size("x")
    assert height == breadth

    def lines_of(phase):
        lines = []
        for c in range(cores):
            for fixed in range(height):
                along_x = [breadth * fixed + i for i in range(breadth)]
                along_y = [breadth * i + fixed for i in range(height)]
                line = along_x if phase == c else along_y
                lines.append([columns * c + i for i in line])
        return lines

    def copy_for_each(value, lines):
        spread = jnp.broadcast_to(value[None], (len(lines[0]), *value.shape))
        return lax.all_to_all(
            spread, ("core", *COLS), 0, 0, axis_index_groups=lines, tiled=True
        )

    sent = jnp.stack([jnp.where(place == 0, t[0], t[1]) for t in (mine, other)])
    left = copy_for_each(copy_for_each(sent, lines_of(0)), lines_of(1))

    held = [(mine, other)]
    for step in range(1, half + 1):
        if step == half:
            known = (plane_ref, core_ref, left, held)
            early = [(i, 0) for i in range(half - 1)]
            totals = products(None, (0, 1), *known, early, [[0, 1], [2, 3], [4, 5], [6]])
            held[-1] = (held[-1][0], settle(held[-1][1], totals.values(), 0))
        elif step == half - 1:
            held[-1] = (held[-1][0], settle(held[-1][1], (), FLOPS))
        perm = ring + back if step < half else back
        held.append(tuple(lax.ppermute(t, ROWS, perm) for t in held[-1]))
    rest = [(i, 1) for i in range(1, half - 1)] + [(half - 1, None)]
    totals = products(totals, (0, 1), *known, rest, [[0, 1], [2, 3], [4, 5], [6]])
    late = [(half, 1)]
    outward = products(totals, (1,), *known, late, [[0]])[1]
    received = lax.ppermute(outward, "core", SWAP)
    total = products(totals, (0,), *known, late, [[0]])[0]
    inflated, sums = pl.pallas_call(
        functools.partial(square_kernel, columns),
        in_specs=[SMEM, SMEM, VMEM, VMEM],
        out_specs=[VMEM, VMEM],
        out_shape=[
            jax.ShapeDtypeStruct((2, width, width), jnp.float32),
            jax.ShapeDtypeStruct((2, width), jnp.float32),
        ],
        compiler_params=params(6),
    )(own, column_ref, total, received)
    sums = lax.all_gather(sums, "core", axis=0).sum(axis=0)
    far = [(z + half) % planes for z in range(planes)]
    parts = lax.all_to_all(
        jnp.broadcast_to(sums[None], (planes, *sums.shape)),
        "z",
        0,
        0,
        axis_index_groups=[far],
        tiled=True,
    )
    scale = float(planes * cores * width)
    out = pl.pallas_call(
        functools.partial(blend_kernel, scale, columns),
        in_specs=[SMEM, SMEM, VMEM, VMEM, VMEM],
        out_specs=VMEM,
        out_shape=jax.ShapeDtypeStruct((2, width, width), jnp.float32),
        compiler_params=params(6),
    )(own, column_ref, tiles, inflated, parts)
    return out[None]


def solution(mesh):
    physical = Mesh(mesh.devices.reshape(16, 2, 4, 4), (*ROWS, *COLS))
    tiled = P(ROWS, COLS, None, None)
    return jax.shard_map(
        on_device,
        mesh=physical,
        in_specs=(tiled, P(ROWS, COLS), P((*ROWS, *COLS), None)),
        out_specs=tiled,
        check_vma=False,
    )
```

```python
import functools

import jax
import jax.numpy as jnp
from jax import lax
from jax.experimental import pallas as pl
from jax.experimental.pallas import tpu as pltpu
from jax.sharding import Mesh, PartitionSpec as P

ROWS = ("z", "core")
COLS = ("y", "x")
SMEM = pl.BlockSpec(memory_space=pltpu.SMEM)
VMEM = pl.BlockSpec(memory_space=pltpu.VMEM)
ANY = pl.BlockSpec(memory_space=pl.ANY)
HBM = pl.BlockSpec(memory_space=pltpu.HBM)
MIB = 1024 * 1024
SWAP = [(0, 1), (1, 0)]
FLOPS = 26 * 10**9


def params(mib):
    return pltpu.CompilerParams(vmem_limit_bytes=mib * MIB)


def order_kernel(columns, own_ref, column_ref, tiles_ref, ordered_ref):
    for place in range(2):
        target = column_ref[0] + columns * place
        first = (own_ref[0] == target).astype(jnp.float32)
        second = (own_ref[1] == target).astype(jnp.float32)
        value = tiles_ref[0].astype(jnp.float32) * first + tiles_ref[1].astype(jnp.float32) * second
        ordered_ref[place] = value.astype(ordered_ref.dtype)


def settle_kernel(*refs):
    del refs


def fetch(plan, guard_ref, start):
    for copies, guard in plan:
        def go(copies=copies):
            for copy in copies:
                copy.start() if start else copy.wait()

        if guard is None:
            go()
        else:
            pl.when(guard_ref[0] == guard)(go)


def product_kernel(planes, rows, groups, plane_ref, core_ref, left_ref, *refs):
    count = 2 * len(planes)
    rights, refs = refs[:count], refs[count:]
    totals, (held, kept, sems) = refs[-3 - len(rows) : -3], refs[-3:]
    carried = len(refs) > 3 + len(rows)
    core = core_ref[0]
    breadth = left_ref.shape[0]
    columns = breadth * breadth
    plan = []
    for i, (distance, guard) in enumerate(planes):
        copies = []
        for j in range(2):
            inner = 2 * (plane_ref[0] + jnp.where(core == 0, -distance, distance))
            inner += jnp.where(core == 0, j, 1 - j)
            place = lax.rem(inner + 2 * columns, columns)
            y, x = place // breadth, lax.rem(place, breadth)
            outer, nested = jnp.where(core == 0, y, x), jnp.where(core == 0, x, y)
            for n, row in enumerate(rows):
                source = left_ref.at[outer, nested, row]
                copies.append(
                    pltpu.make_async_copy(source, held.at[2 * i + j, n], sems.at[2 * i + j, n])
                )
            if len(planes) > 1:
                copies.append(
                    pltpu.make_async_copy(
                        rights[2 * i + j], kept.at[2 * i + j], sems.at[2 * i + j, len(rows)]
                    )
                )
        plan.append((copies, guard))
    for group in groups:
        fetch([plan[i] for i in group], core_ref, True)
    if len(planes) > 1:
        @pl.when(core == int(carried))
        def _():
            for total in totals:
                total[...] = jnp.zeros_like(total)

    width = held.shape[-1]
    for group in groups:
        fetch([plan[i] for i in group], core_ref, False)

        def add(group=group):
            tiles = [2 * i + j for i in group for j in range(2)]
            left = jnp.concatenate(
                [held[i].reshape(len(rows) * width, width) for i in tiles], axis=1
            )
            for column in range(2):
                right = [kept[i, column] if len(planes) > 1 else rights[i][column] for i in tiles]
                right = jnp.concatenate(right, axis=0)
                product = jnp.dot(left, right, preferred_element_type=jnp.float32)
                for n, total in enumerate(totals):
                    total[column] += product[n * width : (n + 1) * width]

        guard = planes[group[0]][1]
        if guard is None:
            add()
        else:
            pl.when(core == guard)(add)


def products(totals, rows, plane, core, left, held, planes, groups):
    width = left.shape[-1]
    tiles = [tile for distance, _ in planes for tile in held[distance]]
    if len(planes) > 1:
        tiles = [pltpu.with_memory_space_constraint(tile, pltpu.HBM) for tile in tiles]
    given = [] if totals is None else [totals[row] for row in rows]
    kernel = functools.partial(product_kernel, planes, rows, groups)
    out = pl.pallas_call(
        kernel,
        in_specs=[SMEM, SMEM, HBM]
        + [HBM if len(planes) > 1 else VMEM] * len(tiles)
        + [VMEM] * len(given),
        out_specs=[VMEM] * len(rows),
        out_shape=[jax.ShapeDtypeStruct((2, width, width), jnp.float32)] * len(rows),
        scratch_shapes=[
            pltpu.VMEM((len(tiles), len(rows), width, width), left.dtype),
            pltpu.VMEM((len(tiles), 2, width, width), left.dtype),
            pltpu.SemaphoreType.DMA((len(tiles), len(rows) + 1)),
        ],
        input_output_aliases={3 + len(tiles) + n: n for n in range(len(given))},
        compiler_params=params(10),
        cost_estimate=pl.CostEstimate(
            flops=4 * len(tiles) * len(rows) * width**3,
            bytes_accessed=4 * len(tiles) * (len(rows) + 2) * width**2,
            transcendentals=0,
        ),
    )(plane, core, left, *tiles, *given)
    return dict(zip(rows, out))


def square_kernel(columns, own_ref, column_ref, mine_ref, other_ref, inflated_ref, sums_ref):
    for place in range(2):
        target = column_ref[0] + columns * place
        kept = (own_ref[0] == target) | (own_ref[1] == target)
        value = mine_ref[place] + other_ref[place]
        value = jnp.where(kept, value * value, 0.0)
        inflated_ref[place] = value
        sums_ref[place : place + 1, :] = jnp.sum(value, axis=0, keepdims=True)


def blend_kernel(scale, columns, own_ref, column_ref, tiles_ref, inflated_ref, parts_ref, out_ref):
    factors = 0.5 * scale / jnp.sum(parts_ref[...], axis=0)
    for slot in range(2):
        tile = tiles_ref[slot].astype(jnp.float32)
        for place in range(2):
            @pl.when(own_ref[slot] == column_ref[0] + columns * place)
            def _():
                out_ref[slot] = 0.5 * tile + inflated_ref[place] * factors[place : place + 1, :]

        @pl.when(own_ref[slot] < 0)
        def _():
            out_ref[slot] = jnp.zeros_like(tile)


def settle(value, after, flops):
    return pl.pallas_call(
        settle_kernel,
        in_specs=[ANY] * (1 + len(after)),
        out_specs=ANY,
        out_shape=jax.ShapeDtypeStruct(value.shape, value.dtype),
        input_output_aliases={0: 0},
        compiler_params=params(1),
        cost_estimate=pl.CostEstimate(flops=flops, bytes_accessed=0, transcendentals=0),
    )(value, *after)


def on_device(flow_tiles, tile_cols, pairs):
    width = flow_tiles.shape[3]
    planes, cores = lax.axis_size("z"), lax.axis_size("core")
    columns = lax.axis_size(COLS)
    plane, core, column = lax.axis_index("z"), lax.axis_index("core"), lax.axis_index(COLS)
    plane_ref, core_ref, column_ref = (
        i.astype(jnp.int32).reshape(1) for i in (plane, core, column)
    )
    own = pltpu.with_memory_space_constraint(tile_cols[0], pltpu.HBM)
    tiles = flow_tiles[0]
    mine = pl.pallas_call(
        functools.partial(order_kernel, columns),
        in_specs=[SMEM, SMEM, VMEM],
        out_specs=VMEM,
        out_shape=jax.ShapeDtypeStruct((2, width, width), tiles.dtype),
        compiler_params=params(4),
    )(own, column_ref, pltpu.with_memory_space_constraint(tiles, pltpu.HBM))
    other = lax.ppermute(mine, "core", SWAP)

    half = planes // 2
    ring = [(2 * z, 2 * ((z + 1) % planes)) for z in range(planes)]
    back = [(2 * z + 1, 2 * ((z - 1) % planes) + 1) for z in range(planes)]
    low = lax.rem(column - 2 * (plane - half + 1) + 2 * columns, 2 * columns)
    place = jnp.where((low < columns) == (core == 0), 0, 1)
    height, breadth = lax.axis_size("y"), lax.axis_size("x")
    assert height == breadth

    def lines_of(phase):
        lines = []
        for c in range(cores):
            for fixed in range(height):
                along_x = [breadth * fixed + i for i in range(breadth)]
                along_y = [breadth * i + fixed for i in range(height)]
                line = along_x if phase == c else along_y
                lines.append([columns * c + i for i in line])
        return lines

    def copy_for_each(value, lines):
        spread = jnp.broadcast_to(value[None], (len(lines[0]), *value.shape))
        return lax.all_to_all(
            spread, ("core", *COLS), 0, 0, axis_index_groups=lines, tiled=True
        )

    sent = jnp.stack([jnp.where(place == 0, t[0], t[1]) for t in (mine, other)])
    left = copy_for_each(copy_for_each(sent, lines_of(0)), lines_of(1))

    held = [(mine, other)]
    for step in range(1, half + 1):
        if step == half:
            known = (plane_ref, core_ref, left, held)
            early = [(i, 0) for i in range(half - 1)]
            totals = products(None, (0, 1), *known, early, [[0, 1], [2, 3], [4, 5], [6]])
            held[-1] = (held[-1][0], settle(held[-1][1], totals.values(), 0))
        elif step == half - 1:
            held[-1] = (held[-1][0], settle(held[-1][1], (), FLOPS))
        perm = ring + back if step < half else back
        held.append(tuple(lax.ppermute(t, ROWS, perm) for t in held[-1]))
    rest = [(i, 1) for i in range(1, half - 1)] + [(half - 1, None)]
    totals = products(totals, (0, 1), *known, rest, [[0, 1], [2, 3], [4, 5], [6]])
    late = [(half, 1)]
    outward = products(totals, (1,), *known, late, [[0]])[1]
    received = lax.ppermute(outward, "core", SWAP)
    total = products(totals, (0,), *known, late, [[0]])[0]
    inflated, sums = pl.pallas_call(
        functools.partial(square_kernel, columns),
        in_specs=[SMEM, SMEM, VMEM, VMEM],
        out_specs=[VMEM, VMEM],
        out_shape=[
            jax.ShapeDtypeStruct((2, width, width), jnp.float32),
            jax.ShapeDtypeStruct((2, width), jnp.float32),
        ],
        compiler_params=params(6),
    )(own, column_ref, total, received)
    sums = lax.all_gather(sums, "core", axis=0).sum(axis=0)
    far = [(z + half) % planes for z in range(planes)]
    parts = lax.all_to_all(
        jnp.broadcast_to(sums[None], (planes, *sums.shape)),
        "z",
        0,
        0,
        axis_index_groups=[far],
        tiled=True,
    )
    scale = float(planes * cores * width)
    out = pl.pallas_call(
        functools.partial(blend_kernel, scale, columns),
        in_specs=[SMEM, SMEM, VMEM, VMEM, VMEM],
        out_specs=VMEM,
        out_shape=jax.ShapeDtypeStruct((2, width, width), jnp.float32),
        compiler_params=params(6),
    )(own, column_ref, tiles, inflated, parts)
    return out[None]


def solution(mesh):
    physical = Mesh(mesh.devices.reshape(16, 2, 4, 4), (*ROWS, *COLS))
    tiled = P(ROWS, COLS, None, None)
    return jax.shard_map(
        on_device,
        mesh=physical,
        in_specs=(tiled, P(ROWS, COLS), P((*ROWS, *COLS), None)),
        out_specs=tiled,
        check_vma=False,
    )
```

```python
import functools

import jax
import jax.numpy as jnp
from jax import lax
from jax.experimental import pallas as pl
from jax.experimental.pallas import tpu as pltpu
from jax.sharding import Mesh, PartitionSpec as P

ROWS = ("z", "core")
COLS = ("y", "x")
SMEM = pl.BlockSpec(memory_space=pltpu.SMEM)
VMEM = pl.BlockSpec(memory_space=pltpu.VMEM)
ANY = pl.BlockSpec(memory_space=pl.ANY)
HBM = pl.BlockSpec(memory_space=pltpu.HBM)
MIB = 1024 * 1024
SWAP = [(0, 1), (1, 0)]
FLOPS = 26 * 10**9


def params(mib):
    return pltpu.CompilerParams(vmem_limit_bytes=mib * MIB)


def order_kernel(columns, own_ref, column_ref, tiles_ref, ordered_ref):
    for place in range(2):
        target = column_ref[0] + columns * place
        first = (own_ref[0] == target).astype(jnp.float32)
        second = (own_ref[1] == target).astype(jnp.float32)
        value = tiles_ref[0].astype(jnp.float32) * first + tiles_ref[1].astype(jnp.float32) * second
        ordered_ref[place] = value.astype(ordered_ref.dtype)


def settle_kernel(*refs):
    del refs


def fetch(plan, guard_ref, start):
    for copies, guard in plan:
        def go(copies=copies):
            for copy in copies:
                copy.start() if start else copy.wait()

        if guard is None:
            go()
        else:
            pl.when(guard_ref[0] == guard)(go)


def product_kernel(planes, rows, groups, plane_ref, core_ref, left_ref, *refs):
    count = 2 * len(planes)
    rights, refs = refs[:count], refs[count:]
    totals, (held, kept, sems) = refs[-3 - len(rows) : -3], refs[-3:]
    carried = len(refs) > 3 + len(rows)
    core = core_ref[0]
    breadth = left_ref.shape[0]
    columns = breadth * breadth
    plan = []
    for i, (distance, guard) in enumerate(planes):
        copies = []
        for j in range(2):
            inner = 2 * (plane_ref[0] + jnp.where(core == 0, -distance, distance))
            inner += jnp.where(core == 0, j, 1 - j)
            place = lax.rem(inner + 2 * columns, columns)
            y, x = place // breadth, lax.rem(place, breadth)
            outer, nested = jnp.where(core == 0, y, x), jnp.where(core == 0, x, y)
            for n, row in enumerate(rows):
                source = left_ref.at[outer, nested, row]
                copies.append(
                    pltpu.make_async_copy(source, held.at[2 * i + j, n], sems.at[2 * i + j, n])
                )
            if len(planes) > 1:
                copies.append(
                    pltpu.make_async_copy(
                        rights[2 * i + j], kept.at[2 * i + j], sems.at[2 * i + j, len(rows)]
                    )
                )
        plan.append((copies, guard))
    for group in groups:
        fetch([plan[i] for i in group], core_ref, True)
    if len(planes) > 1:
        @pl.when(core == int(carried))
        def _():
            for total in totals:
                total[...] = jnp.zeros_like(total)

    width = held.shape[-1]
    for group in groups:
        fetch([plan[i] for i in group], core_ref, False)

        def add(group=group):
            tiles = [2 * i + j for i in group for j in range(2)]
            left = jnp.concatenate(
                [held[i].reshape(len(rows) * width, width) for i in tiles], axis=1
            )
            for column in range(2):
                right = [kept[i, column] if len(planes) > 1 else rights[i][column] for i in tiles]
                right = jnp.concatenate(right, axis=0)
                product = jnp.dot(left, right, preferred_element_type=jnp.float32)
                for n, total in enumerate(totals):
                    total[column] += product[n * width : (n + 1) * width]

        guard = planes[group[0]][1]
        if guard is None:
            add()
        else:
            pl.when(core == guard)(add)


def products(totals, rows, plane, core, left, held, planes, groups):
    width = left.shape[-1]
    tiles = [tile for distance, _ in planes for tile in held[distance]]
    if len(planes) > 1:
        tiles = [pltpu.with_memory_space_constraint(tile, pltpu.HBM) for tile in tiles]
    given = [] if totals is None else [totals[row] for row in rows]
    kernel = functools.partial(product_kernel, planes, rows, groups)
    out = pl.pallas_call(
        kernel,
        in_specs=[SMEM, SMEM, HBM]
        + [HBM if len(planes) > 1 else VMEM] * len(tiles)
        + [VMEM] * len(given),
        out_specs=[VMEM] * len(rows),
        out_shape=[jax.ShapeDtypeStruct((2, width, width), jnp.float32)] * len(rows),
        scratch_shapes=[
            pltpu.VMEM((len(tiles), len(rows), width, width), left.dtype),
            pltpu.VMEM((len(tiles), 2, width, width), left.dtype),
            pltpu.SemaphoreType.DMA((len(tiles), len(rows) + 1)),
        ],
        input_output_aliases={3 + len(tiles) + n: n for n in range(len(given))},
        compiler_params=params(10),
        cost_estimate=pl.CostEstimate(
            flops=4 * len(tiles) * len(rows) * width**3,
            bytes_accessed=4 * len(tiles) * (len(rows) + 2) * width**2,
            transcendentals=0,
        ),
    )(plane, core, left, *tiles, *given)
    return dict(zip(rows, out))


def square_kernel(columns, own_ref, column_ref, mine_ref, other_ref, inflated_ref, sums_ref):
    for place in range(2):
        target = column_ref[0] + columns * place
        kept = (own_ref[0] == target) | (own_ref[1] == target)
        value = mine_ref[place] + other_ref[place]
        value = jnp.where(kept, value * value, 0.0)
        inflated_ref[place] = value
        sums_ref[place : place + 1, :] = jnp.sum(value, axis=0, keepdims=True)


def blend_kernel(scale, columns, own_ref, column_ref, tiles_ref, inflated_ref, parts_ref, out_ref):
    factors = 0.5 * scale / jnp.sum(parts_ref[...], axis=0)
    for slot in range(2):
        tile = tiles_ref[slot].astype(jnp.float32)
        for place in range(2):
            @pl.when(own_ref[slot] == column_ref[0] + columns * place)
            def _():
                out_ref[slot] = 0.5 * tile + inflated_ref[place] * factors[place : place + 1, :]

        @pl.when(own_ref[slot] < 0)
        def _():
            out_ref[slot] = jnp.zeros_like(tile)


def settle(value, after, flops):
    return pl.pallas_call(
        settle_kernel,
        in_specs=[ANY] * (1 + len(after)),
        out_specs=ANY,
        out_shape=jax.ShapeDtypeStruct(value.shape, value.dtype),
        input_output_aliases={0: 0},
        compiler_params=params(1),
        cost_estimate=pl.CostEstimate(flops=flops, bytes_accessed=0, transcendentals=0),
    )(value, *after)


def on_device(flow_tiles, tile_cols, pairs):
    width = flow_tiles.shape[3]
    planes, cores = lax.axis_size("z"), lax.axis_size("core")
    columns = lax.axis_size(COLS)
    plane, core, column = lax.axis_index("z"), lax.axis_index("core"), lax.axis_index(COLS)
    plane_ref, core_ref, column_ref = (
        i.astype(jnp.int32).reshape(1) for i in (plane, core, column)
    )
    own = pltpu.with_memory_space_constraint(tile_cols[0], pltpu.HBM)
    tiles = flow_tiles[0]
    mine = pl.pallas_call(
        functools.partial(order_kernel, columns),
        in_specs=[SMEM, SMEM, VMEM],
        out_specs=VMEM,
        out_shape=jax.ShapeDtypeStruct((2, width, width), tiles.dtype),
        compiler_params=params(4),
    )(own, column_ref, pltpu.with_memory_space_constraint(tiles, pltpu.HBM))
    other = lax.ppermute(mine, "core", SWAP)

    half = planes // 2
    ring = [(2 * z, 2 * ((z + 1) % planes)) for z in range(planes)]
    back = [(2 * z + 1, 2 * ((z - 1) % planes) + 1) for z in range(planes)]
    low = lax.rem(column - 2 * (plane - half + 1) + 2 * columns, 2 * columns)
    place = jnp.where((low < columns) == (core == 0), 0, 1)
    height, breadth = lax.axis_size("y"), lax.axis_size("x")
    assert height == breadth

    def lines_of(phase):
        lines = []
        for c in range(cores):
            for fixed in range(height):
                along_x = [breadth * fixed + i for i in range(breadth)]
                along_y = [breadth * i + fixed for i in range(height)]
                line = along_x if phase == c else along_y
                lines.append([columns * c + i for i in line])
        return lines

    def copy_for_each(value, lines):
        spread = jnp.broadcast_to(value[None], (len(lines[0]), *value.shape))
        return lax.all_to_all(
            spread, ("core", *COLS), 0, 0, axis_index_groups=lines, tiled=True
        )

    sent = jnp.stack([jnp.where(place == 0, t[0], t[1]) for t in (mine, other)])
    left = copy_for_each(copy_for_each(sent, lines_of(0)), lines_of(1))

    held = [(mine, other)]
    for step in range(1, half + 1):
        if step == half:
            known = (plane_ref, core_ref, left, held)
            early = [(i, 0) for i in range(half - 1)]
            totals = products(None, (0, 1), *known, early, [[0, 1], [2, 3], [4, 5], [6]])
            held[-1] = (settle(held[-1][0], totals.values(), 0), held[-1][1])
        elif step == half - 1:
            held[-1] = (held[-1][0], settle(held[-1][1], (), FLOPS))
        perm = ring + back if step < half else back
        held.append(tuple(lax.ppermute(t, ROWS, perm) for t in held[-1]))
    rest = [(i, 1) for i in range(1, half - 1)] + [(half - 1, None)]
    totals = products(totals, (0, 1), *known, rest, [[0, 1], [2, 3], [4, 5], [6]])
    late = [(half, 1)]
    outward = products(totals, (1,), *known, late, [[0]])[1]
    received = lax.ppermute(outward, "core", SWAP)
    total = products(totals, (0,), *known, late, [[0]])[0]
    inflated, sums = pl.pallas_call(
        functools.partial(square_kernel, columns),
        in_specs=[SMEM, SMEM, VMEM, VMEM],
        out_specs=[VMEM, VMEM],
        out_shape=[
            jax.ShapeDtypeStruct((2, width, width), jnp.float32),
            jax.ShapeDtypeStruct((2, width), jnp.float32),
        ],
        compiler_params=params(6),
    )(own, column_ref, total, received)
    sums = lax.all_gather(sums, "core", axis=0).sum(axis=0)
    far = [(z + half) % planes for z in range(planes)]
    parts = lax.all_to_all(
        jnp.broadcast_to(sums[None], (planes, *sums.shape)),
        "z",
        0,
        0,
        axis_index_groups=[far],
        tiled=True,
    )
    scale = float(planes * cores * width)
    out = pl.pallas_call(
        functools.partial(blend_kernel, scale, columns),
        in_specs=[SMEM, SMEM, VMEM, VMEM, VMEM],
        out_specs=VMEM,
        out_shape=jax.ShapeDtypeStruct((2, width, width), jnp.float32),
        compiler_params=params(6),
    )(own, column_ref, tiles, inflated, parts)
    return out[None]


def solution(mesh):
    physical = Mesh(mesh.devices.reshape(16, 2, 4, 4), (*ROWS, *COLS))
    tiled = P(ROWS, COLS, None, None)
    return jax.shard_map(
        on_device,
        mesh=physical,
        in_specs=(tiled, P(ROWS, COLS), P((*ROWS, *COLS), None)),
        out_specs=tiled,
        check_vma=False,
    )
```

```python
import functools

import jax
import jax.numpy as jnp
from jax import lax
from jax.experimental import pallas as pl
from jax.experimental.pallas import tpu as pltpu
from jax.sharding import Mesh, PartitionSpec as P

ROWS = ("z", "core")
COLS = ("y", "x")
SMEM = pl.BlockSpec(memory_space=pltpu.SMEM)
VMEM = pl.BlockSpec(memory_space=pltpu.VMEM)
ANY = pl.BlockSpec(memory_space=pl.ANY)
HBM = pl.BlockSpec(memory_space=pltpu.HBM)
MIB = 1024 * 1024
SWAP = [(0, 1), (1, 0)]
FLOPS = 25 * 10**9


def params(mib):
    return pltpu.CompilerParams(vmem_limit_bytes=mib * MIB)


def order_kernel(columns, own_ref, column_ref, tiles_ref, ordered_ref):
    for place in range(2):
        target = column_ref[0] + columns * place
        first = (own_ref[0] == target).astype(jnp.float32)
        second = (own_ref[1] == target).astype(jnp.float32)
        value = tiles_ref[0].astype(jnp.float32) * first + tiles_ref[1].astype(jnp.float32) * second
        ordered_ref[place] = value.astype(ordered_ref.dtype)


def settle_kernel(*refs):
    del refs


def fetch(plan, guard_ref, start):
    for copies, guard in plan:
        def go(copies=copies):
            for copy in copies:
                copy.start() if start else copy.wait()

        if guard is None:
            go()
        else:
            pl.when(guard_ref[0] == guard)(go)


def product_kernel(planes, rows, groups, plane_ref, core_ref, left_ref, *refs):
    count = 2 * len(planes)
    rights, refs = refs[:count], refs[count:]
    totals, (held, kept, sems) = refs[-3 - len(rows) : -3], refs[-3:]
    carried = len(refs) > 3 + len(rows)
    core = core_ref[0]
    breadth = left_ref.shape[0]
    columns = breadth * breadth
    plan = []
    for i, (distance, guard) in enumerate(planes):
        copies = []
        for j in range(2):
            inner = 2 * (plane_ref[0] + jnp.where(core == 0, -distance, distance))
            inner += jnp.where(core == 0, j, 1 - j)
            place = lax.rem(inner + 2 * columns, columns)
            y, x = place // breadth, lax.rem(place, breadth)
            outer, nested = jnp.where(core == 0, y, x), jnp.where(core == 0, x, y)
            for n, row in enumerate(rows):
                source = left_ref.at[outer, nested, row]
                copies.append(
                    pltpu.make_async_copy(source, held.at[2 * i + j, n], sems.at[2 * i + j, n])
                )
            if len(planes) > 1:
                copies.append(
                    pltpu.make_async_copy(
                        rights[2 * i + j], kept.at[2 * i + j], sems.at[2 * i + j, len(rows)]
                    )
                )
        plan.append((copies, guard))
    for group in groups:
        fetch([plan[i] for i in group], core_ref, True)
    if len(planes) > 1:
        @pl.when(core == int(carried))
        def _():
            for total in totals:
                total[...] = jnp.zeros_like(total)

    width = held.shape[-1]
    for group in groups:
        fetch([plan[i] for i in group], core_ref, False)

        def add(group=group):
            tiles = [2 * i + j for i in group for j in range(2)]
            left = jnp.concatenate(
                [held[i].reshape(len(rows) * width, width) for i in tiles], axis=1
            )
            for column in range(2):
                right = [kept[i, column] if len(planes) > 1 else rights[i][column] for i in tiles]
                right = jnp.concatenate(right, axis=0)
                product = jnp.dot(left, right, preferred_element_type=jnp.float32)
                for n, total in enumerate(totals):
                    total[column] += product[n * width : (n + 1) * width]

        guard = planes[group[0]][1]
        if guard is None:
            add()
        else:
            pl.when(core == guard)(add)


def products(totals, rows, plane, core, left, held, planes, groups):
    width = left.shape[-1]
    tiles = [tile for distance, _ in planes for tile in held[distance]]
    if len(planes) > 1:
        tiles = [pltpu.with_memory_space_constraint(tile, pltpu.HBM) for tile in tiles]
    given = [] if totals is None else [totals[row] for row in rows]
    kernel = functools.partial(product_kernel, planes, rows, groups)
    out = pl.pallas_call(
        kernel,
        in_specs=[SMEM, SMEM, HBM]
        + [HBM if len(planes) > 1 else VMEM] * len(tiles)
        + [VMEM] * len(given),
        out_specs=[VMEM] * len(rows),
        out_shape=[jax.ShapeDtypeStruct((2, width, width), jnp.float32)] * len(rows),
        scratch_shapes=[
            pltpu.VMEM((len(tiles), len(rows), width, width), left.dtype),
            pltpu.VMEM((len(tiles), 2, width, width), left.dtype),
            pltpu.SemaphoreType.DMA((len(tiles), len(rows) + 1)),
        ],
        input_output_aliases={3 + len(tiles) + n: n for n in range(len(given))},
        compiler_params=params(10),
        cost_estimate=pl.CostEstimate(
            flops=4 * len(tiles) * len(rows) * width**3,
            bytes_accessed=4 * len(tiles) * (len(rows) + 2) * width**2,
            transcendentals=0,
        ),
    )(plane, core, left, *tiles, *given)
    return dict(zip(rows, out))


def square_kernel(columns, own_ref, column_ref, mine_ref, other_ref, inflated_ref, sums_ref):
    for place in range(2):
        target = column_ref[0] + columns * place
        kept = (own_ref[0] == target) | (own_ref[1] == target)
        value = mine_ref[place] + other_ref[place]
        value = jnp.where(kept, value * value, 0.0)
        inflated_ref[place] = value
        sums_ref[place : place + 1, :] = jnp.sum(value, axis=0, keepdims=True)


def blend_kernel(scale, columns, own_ref, column_ref, tiles_ref, inflated_ref, parts_ref, out_ref):
    factors = 0.5 * scale / jnp.sum(parts_ref[...], axis=0)
    for slot in range(2):
        tile = tiles_ref[slot].astype(jnp.float32)
        for place in range(2):
            @pl.when(own_ref[slot] == column_ref[0] + columns * place)
            def _():
                out_ref[slot] = 0.5 * tile + inflated_ref[place] * factors[place : place + 1, :]

        @pl.when(own_ref[slot] < 0)
        def _():
            out_ref[slot] = jnp.zeros_like(tile)


def settle(value, after, flops):
    return pl.pallas_call(
        settle_kernel,
        in_specs=[ANY] * (1 + len(after)),
        out_specs=ANY,
        out_shape=jax.ShapeDtypeStruct(value.shape, value.dtype),
        input_output_aliases={0: 0},
        compiler_params=params(1),
        cost_estimate=pl.CostEstimate(flops=flops, bytes_accessed=0, transcendentals=0),
    )(value, *after)


def on_device(flow_tiles, tile_cols, pairs):
    width = flow_tiles.shape[3]
    planes, cores = lax.axis_size("z"), lax.axis_size("core")
    columns = lax.axis_size(COLS)
    plane, core, column = lax.axis_index("z"), lax.axis_index("core"), lax.axis_index(COLS)
    plane_ref, core_ref, column_ref = (
        i.astype(jnp.int32).reshape(1) for i in (plane, core, column)
    )
    own = pltpu.with_memory_space_constraint(tile_cols[0], pltpu.HBM)
    tiles = flow_tiles[0]
    mine = pl.pallas_call(
        functools.partial(order_kernel, columns),
        in_specs=[SMEM, SMEM, VMEM],
        out_specs=VMEM,
        out_shape=jax.ShapeDtypeStruct((2, width, width), tiles.dtype),
        compiler_params=params(4),
    )(own, column_ref, pltpu.with_memory_space_constraint(tiles, pltpu.HBM))
    other = lax.ppermute(mine, "core", SWAP)

    half = planes // 2
    ring = [(2 * z, 2 * ((z + 1) % planes)) for z in range(planes)]
    back = [(2 * z + 1, 2 * ((z - 1) % planes) + 1) for z in range(planes)]
    low = lax.rem(column - 2 * (plane - half + 1) + 2 * columns, 2 * columns)
    place = jnp.where((low < columns) == (core == 0), 0, 1)
    height, breadth = lax.axis_size("y"), lax.axis_size("x")
    assert height == breadth

    def lines_of(phase):
        lines = []
        for c in range(cores):
            for fixed in range(height):
                along_x = [breadth * fixed + i for i in range(breadth)]
                along_y = [breadth * i + fixed for i in range(height)]
                line = along_x if phase == c else along_y
                lines.append([columns * c + i for i in line])
        return lines

    def copy_for_each(value, lines):
        spread = jnp.broadcast_to(value[None], (len(lines[0]), *value.shape))
        return lax.all_to_all(
            spread, ("core", *COLS), 0, 0, axis_index_groups=lines, tiled=True
        )

    sent = jnp.stack([jnp.where(place == 0, t[0], t[1]) for t in (mine, other)])
    left = copy_for_each(copy_for_each(sent, lines_of(0)), lines_of(1))

    held = [(mine, other)]
    for step in range(1, half + 1):
        if step == half:
            known = (plane_ref, core_ref, left, held)
            early = [(i, 0) for i in range(half - 1)]
            totals = products(None, (0, 1), *known, early, [[0, 1], [2, 3], [4, 5], [6]])
            held[-1] = (held[-1][0], settle(held[-1][1], totals.values(), 0))
        elif step == half - 1:
            held[-1] = (held[-1][0], settle(held[-1][1], (), FLOPS))
        perm = ring + back if step < half else back
        held.append(tuple(lax.ppermute(t, ROWS, perm) for t in held[-1]))
    rest = [(i, 1) for i in range(1, half - 1)] + [(half - 1, None)]
    totals = products(totals, (0, 1), *known, rest, [[0, 1], [2, 3], [4, 5], [6]])
    late = [(half, 1)]
    outward = products(totals, (1,), *known, late, [[0]])[1]
    received = lax.ppermute(outward, "core", SWAP)
    total = products(totals, (0,), *known, late, [[0]])[0]
    inflated, sums = pl.pallas_call(
        functools.partial(square_kernel, columns),
        in_specs=[SMEM, SMEM, VMEM, VMEM],
        out_specs=[VMEM, VMEM],
        out_shape=[
            jax.ShapeDtypeStruct((2, width, width), jnp.float32),
            jax.ShapeDtypeStruct((2, width), jnp.float32),
        ],
        compiler_params=params(6),
    )(own, column_ref, total, received)
    sums = lax.all_gather(sums, "core", axis=0).sum(axis=0)
    far = [(z + half) % planes for z in range(planes)]
    parts = lax.all_to_all(
        jnp.broadcast_to(sums[None], (planes, *sums.shape)),
        "z",
        0,
        0,
        axis_index_groups=[far],
        tiled=True,
    )
    scale = float(planes * cores * width)
    out = pl.pallas_call(
        functools.partial(blend_kernel, scale, columns),
        in_specs=[SMEM, SMEM, VMEM, VMEM, VMEM],
        out_specs=VMEM,
        out_shape=jax.ShapeDtypeStruct((2, width, width), jnp.float32),
        compiler_params=params(6),
    )(own, column_ref, tiles, inflated, parts)
    return out[None]


def solution(mesh):
    physical = Mesh(mesh.devices.reshape(16, 2, 4, 4), (*ROWS, *COLS))
    tiled = P(ROWS, COLS, None, None)
    return jax.shard_map(
        on_device,
        mesh=physical,
        in_specs=(tiled, P(ROWS, COLS), P((*ROWS, *COLS), None)),
        out_specs=tiled,
        check_vma=False,
    )
```
